512 devices in a mesh: rep: 64 (over z_lo, y, x), fsdp: 8 (over z_hi, core).
Axes of the slice: x: 4, y: 8, z: 8 (z_hi: 4, z_lo: 2; z = z_hi * 2 + z_lo), core: 2. Of those that a mesh axis runs over, the one named last changes fastest.
Arguments:
- numerator: bfloat16 [64, 2560, 2560], P('rep', None, 'fsdp'), may hold values from -6 to 6
- push_weight: float32 [64], P('rep'), may hold values from 0.5 to 2
- norm_gain: float32 [2560], replicated, may hold values from 0.1 to 1.9
- activations: bfloat16 [2, 45056, 2560], P(None, ('rep', 'fsdp')), may hold values from -40 to 40, as said below
- cotangent: bfloat16 [2, 45056, 2560], P(None, ('rep', 'fsdp')), may hold values from -6 to 6
- step_index: int32 [], replicated, may hold values from 0 to 999
Outputs:
- mixed: bfloat16 [64, 2560, 2560], P('rep', None, 'fsdp')
- new_weight: float32 [64], P('rep')
The draws below stay inside these ranges and needn't reach their ends.
Inputs may be any that keep to these rules, and one draw needn't show every extreme that they name: `activations`: Per-token and per-feature scales vary.
All inputs are finite; a program needn't handle non-finite values.
Results may differ from the reference program's by a relative error of at most 0.0075.
Values may be sent and summed in bfloat16 or wider, within the bound.
No kernel may reach another device: no remote copies, remote signals or barrier semaphores. Data moves between devices by JAX's collectives and lax.ppermute only.
A program may use at most 64 MiB of HBM per device.

```python
import math
import jax
import jax.numpy as jnp
from jax import lax

DW = 2560
HW = 2560
MICRO = 2
MB_DEV = 88
TOKENS_MB = 45056
N_REP = 64
N_FSDP = 8


def draw_activations(key, part):
    key = jax.random.fold_in(key, 11)
    k_base, k_rows, k_cols = jax.random.split(key, 3)
    row_scale = jnp.exp(jax.random.uniform(k_rows, (MICRO, TOKENS_MB, 1), jnp.float32, jnp.log(0.3), jnp.log(3.0)))
    col_scale = jnp.exp(jax.random.uniform(k_cols, (1, 1, DW), jnp.float32, jnp.log(0.3), jnp.log(3.0)))
    base = jnp.clip(jax.random.normal(k_base, (MICRO, TOKENS_MB, DW), jnp.float32), -4.0, 4.0)
    return (base * row_scale * col_scale).astype(jnp.bfloat16)


def shard_levels(key, dims, cuts, smallest, high):
    def one(axis_at, shards_of):
        draws = jax.random.uniform(jax.random.fold_in(jax.random.fold_in(key, 6), axis_at), (shards_of,), jnp.float32, smallest / len(cuts), high / len(cuts))
        return jnp.repeat(jnp.exp(draws), dims[axis_at] // shards_of).reshape((-1,) + (1,) * (len(dims) - axis_at - 1))

    factor_of = one(*cuts[0])
    for cut in cuts[1:]:
        factor_of = factor_of * one(*cut)
    return factor_of


def bell_draw(stream_key, shape, scale, most, shards=(), kind=jnp.bfloat16):
    level = shard_levels(stream_key, shape, shards, -0.22, 0.18) if shards else 1.0
    values = jax.random.normal(stream_key, shape, jnp.float32) * scale * level
    return jnp.minimum(jnp.maximum(values, -most), most).astype(kind)


def setup_inputs(seed: int = 0) -> dict:
    keys = jax.random.split(jax.random.key(seed), 7)
    return {
        "numerator": bell_draw(keys[0], (N_REP, DW, HW), 1.0, 6.0, ((0, 64), (2, 8))),
        "push_weight": jnp.clip(jnp.exp(math.log(2.0) - 1.3862944 * jax.random.uniform(keys[1], (N_REP,), jnp.float32) ** shard_levels(keys[1], (N_REP,), ((0, 64),), -0.2, 0.2)), 0.5, 2.0),
        "norm_gain": jnp.clip(1.0 + 0.18 * jax.random.normal(keys[2], (DW,), jnp.float32), 0.1, 1.9),
        "activations": draw_activations(jax.random.fold_in(keys[6], 71), 0),
        "cotangent": bell_draw(keys[4], (MICRO, TOKENS_MB, HW), 1.0, 6.0, ((1, 512),)),
        "step_index": jax.random.randint(keys[5], (), 0, 1000).astype(jnp.int32),
    }


LEARN_RATE = 1.5
EPSILON = 1e-05

def silu_slope(pre_act):
    sig = jax.nn.sigmoid(pre_act)
    return sig * (1.0 + pre_act * (1.0 - sig))

def reference(numerator, push_weight, norm_gain, activations, cotangent, step_index):
    group = MB_DEV * N_FSDP
    scale = DW ** (-0.5)
    acts = activations.reshape(MICRO, N_REP, group, DW).transpose(1, 0, 2, 3).reshape(N_REP, MICRO * group, DW)
    cots = cotangent.reshape(MICRO, N_REP, group, HW).transpose(1, 0, 2, 3).reshape(N_REP, MICRO * group, HW)

    def one_replica(items):
        inputs, cot_rows, numer, weight = items
        wide = inputs.astype(jnp.float32)
        mean_square = lax.optimization_barrier(jnp.mean(wide * wide, axis=-1, keepdims=True))
        normed = (wide * lax.rsqrt(mean_square + EPSILON) * norm_gain).astype(jnp.bfloat16)
        eff_weight = (numer.astype(jnp.float32) / weight).astype(jnp.bfloat16)
        pre_act = scale * jnp.dot(normed, eff_weight, preferred_element_type=jnp.float32)
        grad_out = (cot_rows.astype(jnp.float32) * silu_slope(pre_act)).astype(jnp.bfloat16)
        grad = scale * jnp.dot(normed.T, grad_out, preferred_element_type=jnp.float32)
        return (LEARN_RATE * grad).astype(jnp.bfloat16)
    updates = lax.map(one_replica, (acts, cots, numerator, push_weight))
    bit_count = N_REP.bit_length() - 1
    hop_size = jnp.left_shift(jnp.int32(1), (step_index % bit_count).astype(jnp.int32))
    source = ((jnp.arange(N_REP, dtype=jnp.int32) - hop_size) % N_REP).astype(jnp.int32)
    local = numerator.astype(jnp.float32) - updates.astype(jnp.float32)
    mixed = (0.5 * local + 0.5 * local[source]).astype(jnp.bfloat16)
    new_weight = 0.5 * (push_weight + push_weight[source])
    return (mixed, new_weight)
```

```python
from functools import partial

import jax
import jax.numpy as jnp
from jax import lax
from jax.experimental import pallas as pl
from jax.experimental.pallas import tpu as pltpu
from jax.sharding import PartitionSpec as P

DW = 2560
LEARN_RATE = 1.5
EPSILON = 1e-05
SCALE = DW ** (-0.5)
LANES = 128
CHUNKS = (512, 768, 768, 512)
VMEM = 48 * 2**20


def pack_cotangent(cot_t, parts):
    cols, tokens = cot_t.shape
    cot_t = cot_t.reshape(parts, cols // parts, tokens)
    half = cols // parts // 2
    rest = cot_t[:, :, LANES:]
    gap = jnp.zeros((parts, half, LANES - 2 * (tokens - LANES)), cot_t.dtype)
    folded = jnp.concatenate([rest[:, :half], rest[:, half:], gap], axis=2)
    return jnp.concatenate([cot_t[:, :, :LANES], folded], axis=1)


def grad_out_kernel(weight_ref, tokens_ref, cot_ref, out_ref):
    cols, count = out_ref.shape[1:]
    half, rest = cols // 2, count - LANES
    pre_act = SCALE * lax.dot_general(
        weight_ref[...], tokens_ref[...], (((1,), (1,)), ((), ())), preferred_element_type=jnp.float32
    )
    sig = jax.nn.sigmoid(pre_act)
    slope = sig * (1.0 + pre_act * (1.0 - sig))
    cot = cot_ref[0]
    head = cot[:cols].astype(jnp.float32)
    tail = cot[cols:].astype(jnp.float32)
    out_ref[0, :, :LANES] = (head * slope[:, :LANES]).astype(jnp.bfloat16)
    out_ref[0, :half, LANES:] = (tail[:, :rest] * slope[:half, LANES:]).astype(jnp.bfloat16)
    out_ref[0, half:, LANES:] = (tail[:, rest : 2 * rest] * slope[half:, LANES:]).astype(jnp.bfloat16)


def grad_out(weight_t, tokens, packed):
    parts, rows = packed.shape[:2]
    cols = weight_t.shape[0]
    count = tokens.shape[0] // parts
    return pl.pallas_call(
        grad_out_kernel,
        grid=(parts,),
        in_specs=[
            pl.BlockSpec((cols, DW), lambda i: (0, 0)),
            pl.BlockSpec((count, DW), lambda i: (i, 0)),
            pl.BlockSpec((1, rows, LANES), lambda i: (i, 0, 0)),
        ],
        out_specs=pl.BlockSpec((1, cols, count), lambda i: (i, 0, 0)),
        out_shape=jax.ShapeDtypeStruct((parts, cols, count), jnp.bfloat16),
        compiler_params=pltpu.CompilerParams(vmem_limit_bytes=VMEM),
        cost_estimate=pl.CostEstimate(
            flops=2 * cols * DW * count * parts, bytes_accessed=2 * DW * count * parts, transcendentals=0
        ),
    )(weight_t, tokens, packed)


def local_kernel(grad_out_ref, tokens_ref, numer_ref, out_ref):
    parts, _, count = grad_out_ref.shape
    total = jnp.zeros(out_ref.shape, jnp.float32)
    for part in range(parts):
        total += jnp.dot(
            grad_out_ref[part], tokens_ref[part * count : (part + 1) * count], preferred_element_type=jnp.float32
        )
    update = (LEARN_RATE * (SCALE * total)).astype(jnp.bfloat16)
    out_ref[...] = (numer_ref[...].astype(jnp.float32) - update.astype(jnp.float32)).astype(jnp.bfloat16)


def local_chunk(grad_out_t, tokens, numer_t, first, width, tile=256):
    parts, cols, count = grad_out_t.shape
    rows = tokens.shape[0]
    offset = first // tile
    return pl.pallas_call(
        local_kernel,
        grid=(width // tile,),
        in_specs=[
            pl.BlockSpec((parts, cols, count), lambda i: (0, 0, 0)),
            pl.BlockSpec((rows, tile), lambda i: (0, i + offset)),
            pl.BlockSpec((cols, tile), lambda i: (0, i + offset)),
        ],
        out_specs=pl.BlockSpec((cols, tile), lambda i: (0, i)),
        out_shape=jax.ShapeDtypeStruct((cols, width), jnp.bfloat16),
        compiler_params=pltpu.CompilerParams(vmem_limit_bytes=VMEM),
        cost_estimate=pl.CostEstimate(
            flops=2 * cols * rows * width, bytes_accessed=2 * rows * width, transcendentals=0
        ),
    )(grad_out_t, tokens, numer_t)


def route(distance):
    devices = range(lax.axis_size("rep"))
    return [((i - distance) % len(devices), i) for i in devices]


def mix_with(hop_size, grad_out_t, tokens, numer_t, weight):
    pieces, first = [], 0
    for width in CHUNKS:
        local = local_chunk(grad_out_t, tokens, numer_t, first, width)
        partner = lax.ppermute(local, "rep", route(hop_size))
        pieces.append((0.5 * local.astype(jnp.float32) + 0.5 * partner.astype(jnp.float32)).astype(jnp.bfloat16))
        first += width
    new_weight = 0.5 * (weight + lax.ppermute(weight, "rep", route(hop_size)))
    return jnp.concatenate(pieces, axis=1), new_weight


def on_device(numerator, push_weight, norm_gain, activations, cotangent, step_index):
    parts = lax.axis_size("fsdp")
    wide = activations.astype(jnp.float32)
    mean_square = jnp.mean(wide * wide, axis=-1, keepdims=True)
    normed = (wide * lax.rsqrt(mean_square + EPSILON) * norm_gain).astype(jnp.bfloat16)
    tokens = lax.all_gather(normed.reshape(-1, DW), "fsdp", axis=0, tiled=True)
    packed = pack_cotangent(cotangent.reshape(-1, cotangent.shape[2]).T, parts)
    packed = lax.all_to_all(packed, "fsdp", split_axis=0, concat_axis=0, tiled=True)
    numer_t = numerator[0].T
    weight_t = (numer_t.astype(jnp.float32) / push_weight[0]).astype(jnp.bfloat16)
    grad_out_t = grad_out(weight_t, tokens, packed)
    bit_count = lax.axis_size("rep").bit_length() - 1
    branches = [partial(mix_with, 2**bit) for bit in range(bit_count)]
    mixed_t, new_weight = lax.switch(
        step_index % bit_count, branches, grad_out_t, tokens, numer_t, push_weight
    )
    return mixed_t.T[None], new_weight


def solution(mesh):
    placed = (
        P("rep", None, "fsdp"),
        P("rep"),
        P(),
        P(None, ("rep", "fsdp"), None),
        P(None, ("rep", "fsdp"), None),
        P(),
    )
    return jax.shard_map(
        on_device,
        mesh=mesh,
        in_specs=placed,
        out_specs=(P("rep", None, "fsdp"), P("rep")),
        check_vma=False,
    )
```

```python
from functools import partial

import jax
import jax.numpy as jnp
from jax import lax
from jax.experimental import pallas as pl
from jax.experimental.pallas import tpu as pltpu
from jax.sharding import PartitionSpec as P

DW = 2560
LEARN_RATE = 1.5
EPSILON = 1e-05
SCALE = DW ** (-0.5)
LANES = 128
CHUNKS = (512, 768, 768, 512)
VMEM = 48 * 2**20


def pack_cotangent(cot_t, parts):
    cols, tokens = cot_t.shape
    cot_t = cot_t.reshape(parts, cols // parts, tokens)
    half = cols // parts // 2
    rest = cot_t[:, :, LANES:]
    gap = jnp.zeros((parts, half, LANES - 2 * (tokens - LANES)), cot_t.dtype)
    folded = jnp.concatenate([rest[:, :half], rest[:, half:], gap], axis=2)
    return jnp.concatenate([cot_t[:, :, :LANES], folded], axis=1)


def norm_kernel(tokens_ref, gain_ref, out_ref):
    wide = tokens_ref[...].astype(jnp.float32)
    mean_square = jnp.mean(wide * wide, axis=-1, keepdims=True)
    out_ref[...] = (wide * lax.rsqrt(mean_square + EPSILON) * gain_ref[...]).astype(jnp.bfloat16)


def norm(tokens, gain):
    return pl.pallas_call(
        norm_kernel,
        out_shape=jax.ShapeDtypeStruct(tokens.shape, jnp.bfloat16),
        compiler_params=pltpu.CompilerParams(vmem_limit_bytes=VMEM),
        cost_estimate=pl.CostEstimate(flops=8 * tokens.size, bytes_accessed=4 * tokens.size, transcendentals=0),
    )(tokens, gain[None])


def once_there(array, *others):
    whole = pl.BlockSpec(memory_space=pl.ANY)
    return pl.pallas_call(
        lambda *refs: None,
        grid=(1,),
        in_specs=[whole] + [pl.BlockSpec((1, 16, LANES), lambda i: (0, 0, 0))] * len(others),
        out_specs=whole,
        out_shape=jax.ShapeDtypeStruct(array.shape, array.dtype),
        input_output_aliases={0: 0},
    )(array, *others)


def to_chip(values, step):
    count = lax.axis_size("fsdp")
    route = [(i, (i // 2 + (-step if i % 2 else step)) % (count // 2) * 2 + i % 2) for i in range(count)]
    return lax.ppermute(values, "fsdp", route)


def to_core(values):
    return lax.ppermute(values, "fsdp", [(i, i ^ 1) for i in range(lax.axis_size("fsdp"))])


def grad_out_kernel(ids_ref, weight_ref, cot_ref, *refs):
    out_ref = refs[-1]
    _, cols, count = out_ref.shape
    half, rest = cols // 2, count - LANES
    for i in range(out_ref.shape[0]):
        pre_act = SCALE * lax.dot_general(
            weight_ref[...], refs[i][...], (((1,), (1,)), ((), ())), preferred_element_type=jnp.float32
        )
        sig = jax.nn.sigmoid(pre_act)
        slope = sig * (1.0 + pre_act * (1.0 - sig))
        cot = cot_ref[ids_ref[i]]
        head = cot[:cols].astype(jnp.float32)
        tail = cot[cols:].astype(jnp.float32)
        out_ref[i, :, :LANES] = (head * slope[:, :LANES]).astype(jnp.bfloat16)
        out_ref[i, :half, LANES:] = (tail[:, :rest] * slope[:half, LANES:]).astype(jnp.bfloat16)
        out_ref[i, half:, LANES:] = (tail[:, rest : 2 * rest] * slope[half:, LANES:]).astype(jnp.bfloat16)


def grad_out(weight_t, packed, sources, blocks):
    cols, tokens = weight_t.shape[0], blocks[0].shape[0]
    vmem = pl.BlockSpec(memory_space=pltpu.VMEM)
    return pl.pallas_call(
        grad_out_kernel,
        in_specs=[pl.BlockSpec(memory_space=pltpu.SMEM)] + [vmem] * (2 + len(blocks)),
        out_specs=vmem,
        out_shape=jax.ShapeDtypeStruct((len(blocks), cols, tokens), jnp.bfloat16),
        compiler_params=pltpu.CompilerParams(vmem_limit_bytes=VMEM),
        cost_estimate=pl.CostEstimate(
            flops=2 * cols * DW * tokens * len(blocks), bytes_accessed=2 * DW * tokens * len(blocks), transcendentals=0
        ),
    )(jnp.stack(sources), weight_t, packed, *blocks)


def local_kernel(groups, *refs):
    numer_ref, out_ref = refs[-2:]
    tokens_refs = refs[groups:-2]
    total, block = jnp.zeros(out_ref.shape, jnp.float32), 0
    for grad_out_ref in refs[:groups]:
        for i in range(grad_out_ref.shape[0]):
            total += jnp.dot(grad_out_ref[i], tokens_refs[block][...], preferred_element_type=jnp.float32)
            block += 1
    update = (LEARN_RATE * (SCALE * total)).astype(jnp.bfloat16)
    out_ref[...] = (numer_ref[...].astype(jnp.float32) - update.astype(jnp.float32)).astype(jnp.bfloat16)


def local_chunk(grads, blocks, numer_t, first, width, tile=256):
    cols = numer_t.shape[0]
    tokens = blocks[0].shape[0]
    offset = first // tile
    return pl.pallas_call(
        partial(local_kernel, len(grads)),
        grid=(width // tile,),
        in_specs=[pl.BlockSpec(g.shape, lambda i: (0, 0, 0)) for g in grads]
        + [pl.BlockSpec((tokens, tile), lambda i: (0, i + offset))] * len(blocks)
        + [pl.BlockSpec((cols, tile), lambda i: (0, i + offset))],
        out_specs=pl.BlockSpec((cols, tile), lambda i: (0, i)),
        out_shape=jax.ShapeDtypeStruct((cols, width), jnp.bfloat16),
        compiler_params=pltpu.CompilerParams(vmem_limit_bytes=VMEM),
        cost_estimate=pl.CostEstimate(
            flops=2 * cols * tokens * len(blocks) * width,
            bytes_accessed=2 * tokens * len(blocks) * width,
            transcendentals=0,
        ),
    )(*grads, *blocks, numer_t)


def route(distance):
    devices = range(lax.axis_size("rep"))
    return [((i - distance) % len(devices), i) for i in devices]


def mix_with(hop_size, grads, blocks, numer_t, weight):
    pieces, first = [], 0
    for width in CHUNKS:
        local = local_chunk(grads, blocks, numer_t, first, width)
        partner = lax.ppermute(local, "rep", route(hop_size))
        pieces.append((0.5 * local.astype(jnp.float32) + 0.5 * partner.astype(jnp.float32)).astype(jnp.bfloat16))
        first += width
    new_weight = 0.5 * (weight + lax.ppermute(weight, "rep", route(hop_size)))
    return jnp.concatenate(pieces, axis=1), new_weight


def on_device(numerator, push_weight, norm_gain, activations, cotangent, step_index):
    count = lax.axis_size("fsdp")
    me = lax.axis_index("fsdp")
    core = me % 2
    ahead, back, far = ((me + step * (1 - 2 * core) + count) % count for step in (2, -2, 4))
    packed = pack_cotangent(cotangent.reshape(-1, cotangent.shape[2]).T, count)
    packed = lax.all_to_all(packed, "fsdp", split_axis=0, concat_axis=0, tiled=True)
    own = norm(activations.reshape(-1, DW), norm_gain)
    first, second = to_chip(own, 1), to_chip(own, -1)
    first = once_there(first, packed)
    third = to_chip(first, 1)
    numer_t = numerator[0].T
    weight_t = (numer_t.astype(jnp.float32) / push_weight[0]).astype(jnp.bfloat16)
    held = [((me, me ^ 1), own), ((back, ahead ^ 1), first), ((ahead, back ^ 1), second)]
    blocks, grads = [], []
    for sources, block in held:
        pair = (block, to_core(block))
        blocks += pair
        grads.append(grad_out(weight_t, packed, sources, pair))
    third = once_there(third, *grads)
    for source, block in ((far, third), (far ^ 1, to_core(third))):
        blocks.append(block)
        grads.append(grad_out(weight_t, packed, (source,), (block,)))
    bit_count = lax.axis_size("rep").bit_length() - 1
    branches = [partial(mix_with, 2**bit) for bit in range(bit_count)]
    mixed_t, new_weight = lax.switch(
        step_index % bit_count, branches, grads, blocks, numer_t, push_weight
    )
    return mixed_t.T[None], new_weight


def solution(mesh):
    placed = (
        P("rep", None, "fsdp"),
        P("rep"),
        P(),
        P(None, ("rep", "fsdp"), None),
        P(None, ("rep", "fsdp"), None),
        P(),
    )
    return jax.shard_map(
        on_device,
        mesh=mesh,
        in_specs=placed,
        out_specs=(P("rep", None, "fsdp"), P("rep")),
        check_vma=False,
    )
```

```python
from functools import partial

import jax
import jax.numpy as jnp
from jax import lax
from jax.experimental import pallas as pl
from jax.experimental.pallas import tpu as pltpu
from jax.sharding import PartitionSpec as P

DW = 2560
LEARN_RATE = 1.5
EPSILON = 1e-05
SCALE = DW ** (-0.5)
LANES = 128
CHUNKS = (512, 768, 768, 512)
VMEM = 12 * 2**20


def pack_cotangent(cot_t, parts):
    cols, tokens = cot_t.shape
    cot_t = cot_t.reshape(parts, cols // parts, tokens)
    half = cols // parts // 2
    rest = cot_t[:, :, LANES:]
    gap = jnp.zeros((parts, half, LANES - 2 * (tokens - LANES)), cot_t.dtype)
    folded = jnp.concatenate([rest[:, :half], rest[:, half:], gap], axis=2)
    return jnp.concatenate([cot_t[:, :, :LANES], folded], axis=1)


def norm_kernel(tokens_ref, gain_ref, out_ref):
    wide = tokens_ref[...].astype(jnp.float32)
    mean_square = jnp.mean(wide * wide, axis=-1, keepdims=True)
    out_ref[...] = (wide * lax.rsqrt(mean_square + EPSILON) * gain_ref[...]).astype(jnp.bfloat16)


def norm(tokens, gain):
    return pl.pallas_call(
        norm_kernel,
        out_shape=jax.ShapeDtypeStruct(tokens.shape, jnp.bfloat16),
        compiler_params=pltpu.CompilerParams(vmem_limit_bytes=VMEM),
        cost_estimate=pl.CostEstimate(flops=8 * tokens.size, bytes_accessed=4 * tokens.size, transcendentals=0),
    )(tokens, gain[None])


def copy_kernel(array_ref, token_ref, out_ref):
    out_ref[...] = array_ref[...]


def copy_after(array, token):
    return pl.pallas_call(
        copy_kernel,
        grid=(1,),
        in_specs=[pl.BlockSpec(array.shape, lambda i: (0, 0)), pl.BlockSpec((1, 16, LANES), lambda i: (0, 0, 0))],
        out_specs=pl.BlockSpec(array.shape, lambda i: (0, 0)),
        out_shape=jax.ShapeDtypeStruct(array.shape, array.dtype),
        compiler_params=pltpu.CompilerParams(vmem_limit_bytes=VMEM),
    )(array, token)


def once_there(array, *tokens):
    whole = pl.BlockSpec(memory_space=pl.ANY)
    return pl.pallas_call(
        lambda *refs: None,
        in_specs=[whole] + [pl.BlockSpec(memory_space=pltpu.VMEM)] * len(tokens),
        out_specs=whole,
        out_shape=jax.ShapeDtypeStruct(array.shape, array.dtype),
        input_output_aliases={0: 0},
        compiler_params=pltpu.CompilerParams(vmem_limit_bytes=VMEM),
    )(array, *tokens)


def to_chip(values, step):
    count = lax.axis_size("fsdp")
    route = [(i, (i // 2 + (-step if i % 2 else step)) % (count // 2) * 2 + i % 2) for i in range(count)]
    return lax.ppermute(values, "fsdp", route)


def to_core(values):
    return lax.ppermute(values, "fsdp", [(i, i ^ 1) for i in range(lax.axis_size("fsdp"))])


def grad_out_kernel(ids_ref, weight_ref, cot_ref, *refs):
    count = len(refs) - 4
    blocks, (out_ref, token_ref, held, sems) = refs[:count], refs[count:]
    _, cols, tokens = out_ref.shape
    half, rest = cols // 2, tokens - LANES
    copies = [pltpu.make_async_copy(block, held.at[i], sems.at[i]) for i, block in enumerate(blocks)]
    for copy in copies:
        copy.start()
    token_ref[...] = jnp.zeros(token_ref.shape, token_ref.dtype)
    for i, copy in enumerate(copies):
        copy.wait()
        pre_act = SCALE * lax.dot_general(
            weight_ref[...], held[i], (((1,), (1,)), ((), ())), preferred_element_type=jnp.float32
        )
        sig = jax.nn.sigmoid(pre_act)
        slope = sig * (1.0 + pre_act * (1.0 - sig))
        cot = cot_ref[ids_ref[i]]
        head = cot[:cols].astype(jnp.float32)
        tail = cot[cols:].astype(jnp.float32)
        out_ref[i, :, :LANES] = (head * slope[:, :LANES]).astype(jnp.bfloat16)
        out_ref[i, :half, LANES:] = (tail[:, :rest] * slope[:half, LANES:]).astype(jnp.bfloat16)
        out_ref[i, half:, LANES:] = (tail[:, rest : 2 * rest] * slope[half:, LANES:]).astype(jnp.bfloat16)


def grad_out(weight_t, packed, sources, blocks):
    cols, tokens = weight_t.shape[0], blocks[0].shape[0]
    vmem, whole = pl.BlockSpec(memory_space=pltpu.VMEM), pl.BlockSpec(memory_space=pl.ANY)
    return pl.pallas_call(
        grad_out_kernel,
        in_specs=[pl.BlockSpec(memory_space=pltpu.SMEM), vmem, vmem] + [whole] * len(blocks),
        out_specs=(vmem, vmem),
        out_shape=(
            jax.ShapeDtypeStruct((len(blocks), cols, tokens), jnp.bfloat16),
            jax.ShapeDtypeStruct((8, LANES), jnp.float32),
        ),
        scratch_shapes=[
            pltpu.VMEM((len(blocks), tokens, DW), jnp.bfloat16),
            pltpu.SemaphoreType.DMA((len(blocks),)),
        ],
        compiler_params=pltpu.CompilerParams(vmem_limit_bytes=VMEM),
        cost_estimate=pl.CostEstimate(flops=0, bytes_accessed=0, transcendentals=0),
    )(jnp.stack(sources), weight_t, packed, *blocks)


def local_kernel(groups, blocks, first, *refs):
    grads, blocks, (numer_ref, weight_ref) = refs[:groups], refs[groups : groups + blocks], refs[groups + blocks :][:2]
    out_ref, weight_out_ref, held, numer, sems = refs[-5:]
    width, tile = out_ref.shape[1], 256
    columns = pl.ds(first, width)
    copies = [pltpu.make_async_copy(block.at[:, columns], held.at[i], sems.at[i]) for i, block in enumerate(blocks)]
    copies.append(pltpu.make_async_copy(numer_ref.at[:, columns], numer, sems.at[len(blocks)]))
    for copy in copies:
        copy.start()
    weight_out_ref[0] = weight_ref[0]
    for copy in copies:
        copy.wait()
    terms = [grad_ref[i] for grad_ref in grads for i in range(grad_ref.shape[0])]
    for at in range(0, width, tile):
        part = slice(at, at + tile)
        total = jnp.zeros((out_ref.shape[0], tile), jnp.float32)
        for i, term in enumerate(terms):
            total += jnp.dot(term, held[i, :, part], preferred_element_type=jnp.float32)
        update = (LEARN_RATE * (SCALE * total)).astype(jnp.bfloat16)
        out_ref[:, part] = (numer[:, part].astype(jnp.float32) - update.astype(jnp.float32)).astype(jnp.bfloat16)


def local_chunk(grads, blocks, numer_t, weight, first, width):
    cols = numer_t.shape[0]
    tokens = blocks[0].shape[0]
    vmem, smem = pl.BlockSpec(memory_space=pltpu.VMEM), pl.BlockSpec(memory_space=pltpu.SMEM)
    whole = pl.BlockSpec(memory_space=pl.ANY)
    return pl.pallas_call(
        partial(local_kernel, len(grads), len(blocks), first),
        in_specs=[vmem] * len(grads) + [whole] * (len(blocks) + 1) + [smem],
        out_specs=(vmem, smem),
        out_shape=(jax.ShapeDtypeStruct((cols, width), jnp.bfloat16), jax.ShapeDtypeStruct((1,), jnp.float32)),
        scratch_shapes=[
            pltpu.VMEM((len(blocks), tokens, width), jnp.bfloat16),
            pltpu.VMEM((cols, width), jnp.bfloat16),
            pltpu.SemaphoreType.DMA((len(blocks) + 1,)),
        ],
        compiler_params=pltpu.CompilerParams(vmem_limit_bytes=VMEM),
        cost_estimate=pl.CostEstimate(flops=0, bytes_accessed=0, transcendentals=0),
    )(*grads, *blocks, numer_t, weight)


def route(distance):
    devices = range(lax.axis_size("rep"))
    return [((i - distance) % len(devices), i) for i in devices]


def mix_with(hop_size, grads, blocks, numer_t, weight):
    pieces, weights, first = [], [], 0
    for width in CHUNKS:
        local, handed_on = local_chunk(grads, blocks, numer_t, weight, first, width)
        weights.append(handed_on)
        partner = lax.ppermute(local, "rep", route(hop_size))
        pieces.append((0.5 * local.astype(jnp.float32) + 0.5 * partner.astype(jnp.float32)).astype(jnp.bfloat16))
        first += width
    new_weight = 0.5 * (weight + lax.ppermute(weights[1], "rep", route(hop_size)))
    return jnp.concatenate(pieces, axis=1), new_weight


def on_device(numerator, push_weight, norm_gain, activations, cotangent, step_index):
    count = lax.axis_size("fsdp")
    me = lax.axis_index("fsdp")
    core = me % 2
    ahead, back, far = ((me + step * (1 - 2 * core) + count) % count for step in (2, -2, 4))
    packed = pack_cotangent(cotangent.reshape(-1, cotangent.shape[2]).T, count)
    packed = lax.all_to_all(packed, "fsdp", split_axis=0, concat_axis=0, tiled=True)
    own = norm(activations.reshape(-1, DW), norm_gain)
    first = to_chip(own, 1)
    second = to_chip(copy_after(own, packed), -1)
    third = to_chip(first, 1)
    numer_t = numerator[0].T
    weight_t = (numer_t.astype(jnp.float32) / push_weight[0]).astype(jnp.bfloat16)
    held = [((me, me ^ 1), own), ((back, ahead ^ 1), first), ((ahead, back ^ 1), second)]
    blocks, grads, tokens = [], [], []
    for sources, block in held:
        pair = (block, to_core(block))
        blocks += pair
        grad, token = grad_out(weight_t, packed, sources, pair)
        grads.append(grad)
        tokens.append(token)
    third = once_there(third, *tokens)
    for source, block in ((far, third), (far ^ 1, to_core(third))):
        blocks.append(block)
        grads.append(grad_out(weight_t, packed, (source,), (block,))[0])
    bit_count = lax.axis_size("rep").bit_length() - 1
    branches = [partial(mix_with, 2**bit) for bit in range(bit_count)]
    mixed_t, new_weight = lax.switch(
        step_index % bit_count, branches, grads, blocks, numer_t, push_weight
    )
    return mixed_t.T[None], new_weight


def solution(mesh):
    placed = (
        P("rep", None, "fsdp"),
        P("rep"),
        P(),
        P(None, ("rep", "fsdp"), None),
        P(None, ("rep", "fsdp"), None),
        P(),
    )
    return jax.shard_map(
        on_device,
        mesh=mesh,
        in_specs=placed,
        out_specs=(P("rep", None, "fsdp"), P("rep")),
        check_vma=False,
    )
```

```python
from functools import partial

import jax
import jax.numpy as jnp
from jax import lax
from jax.experimental import pallas as pl
from jax.experimental.pallas import tpu as pltpu
from jax.sharding import PartitionSpec as P

DW = 2560
LEARN_RATE = 1.5
EPSILON = 1e-05
SCALE = DW ** (-0.5)
LANES = 128
CHUNKS = (512, 768, 768, 512)
VMEM = 12 * 2**20
EARLY_VMEM = 24 * 2**20
HIDDEN = pl.CostEstimate(flops=1, bytes_accessed=1, transcendentals=0)


def pack_cotangent(cot_t, parts):
    cols, tokens = cot_t.shape
    cot_t = cot_t.reshape(parts, cols // parts, tokens)
    half = cols // parts // 2
    rest = cot_t[:, :, LANES:]
    gap = jnp.zeros((parts, half, LANES - 2 * (tokens - LANES)), cot_t.dtype)
    folded = jnp.concatenate([rest[:, :half], rest[:, half:], gap], axis=2)
    return jnp.concatenate([cot_t[:, :, :LANES], folded], axis=1)


def norm_kernel(tokens_ref, gain_ref, out_ref):
    wide = tokens_ref[...].astype(jnp.float32)
    mean_square = jnp.mean(wide * wide, axis=-1, keepdims=True)
    out_ref[...] = (wide * lax.rsqrt(mean_square + EPSILON) * gain_ref[...]).astype(jnp.bfloat16)


def norm(tokens, gain):
    return pl.pallas_call(
        norm_kernel,
        out_shape=jax.ShapeDtypeStruct(tokens.shape, jnp.bfloat16),
        compiler_params=pltpu.CompilerParams(vmem_limit_bytes=VMEM),
        cost_estimate=pl.CostEstimate(flops=8 * tokens.size, bytes_accessed=4 * tokens.size, transcendentals=0),
    )(tokens, gain[None])


def corner(array):
    return pl.BlockSpec((1,) * (array.ndim - 2) + (16, LANES), lambda i: (0,) * array.ndim)


def copy_kernel(array_ref, *refs):
    refs[-1][...] = array_ref[...]


def copy_after(array, token, *scalars):
    whole = pl.BlockSpec(array.shape, lambda i: (0,) * array.ndim)
    return pl.pallas_call(
        copy_kernel,
        grid=(1,),
        in_specs=[whole, corner(token)] + [pl.BlockSpec(memory_space=pltpu.SMEM)] * len(scalars),
        out_specs=whole,
        out_shape=jax.ShapeDtypeStruct(array.shape, array.dtype),
        compiler_params=pltpu.CompilerParams(vmem_limit_bytes=VMEM),
        cost_estimate=HIDDEN,
    )(array, token, *scalars)


def once_there(array, token):
    whole = pl.BlockSpec(memory_space=pl.ANY)
    return pl.pallas_call(
        lambda *refs: None,
        in_specs=[whole, pl.BlockSpec(memory_space=pltpu.VMEM)],
        out_specs=whole,
        out_shape=jax.ShapeDtypeStruct(array.shape, array.dtype),
        input_output_aliases={0: 0},
        compiler_params=pltpu.CompilerParams(vmem_limit_bytes=VMEM),
        cost_estimate=HIDDEN,
    )(array, token)


def scalar_kernel(value_ref, token_ref, out_ref):
    out_ref[0] = value_ref[0]


def scalar_after(value, token):
    smem = pl.BlockSpec(memory_space=pltpu.SMEM)
    return pl.pallas_call(
        scalar_kernel,
        grid=(1,),
        in_specs=[smem, corner(token)],
        out_specs=smem,
        out_shape=jax.ShapeDtypeStruct(value.shape, value.dtype),
        cost_estimate=HIDDEN,
    )(value, token)


def to_chip(values, step):
    count = lax.axis_size("fsdp")
    route = [(i, (i // 2 + (-step if i % 2 else step)) % (count // 2) * 2 + i % 2) for i in range(count)]
    return lax.ppermute(values, "fsdp", route)


def to_core(values):
    return lax.ppermute(values, "fsdp", [(i, i ^ 1) for i in range(lax.axis_size("fsdp"))])


def grad_out_kernel(ids_ref, weight_ref, cot_ref, *refs):
    count = len(refs) - 4
    blocks, (out_ref, token_ref, held, sems) = refs[:count], refs[count:]
    _, cols, tokens = out_ref.shape
    half, rest = cols // 2, tokens - LANES
    copies = [pltpu.make_async_copy(block, held.at[i], sems.at[i]) for i, block in enumerate(blocks)]
    for copy in copies:
        copy.start()
    token_ref[...] = jnp.zeros(token_ref.shape, token_ref.dtype)
    for i, copy in enumerate(copies):
        copy.wait()
        pre_act = SCALE * lax.dot_general(
            weight_ref[...], held[i], (((1,), (1,)), ((), ())), preferred_element_type=jnp.float32
        )
        sig = jax.nn.sigmoid(pre_act)
        slope = sig * (1.0 + pre_act * (1.0 - sig))
        cot = cot_ref[ids_ref[i]]
        head = cot[:cols].astype(jnp.float32)
        tail = cot[cols:].astype(jnp.float32)
        out_ref[i, :, :LANES] = (head * slope[:, :LANES]).astype(jnp.bfloat16)
        out_ref[i, :half, LANES:] = (tail[:, :rest] * slope[:half, LANES:]).astype(jnp.bfloat16)
        out_ref[i, half:, LANES:] = (tail[:, rest : 2 * rest] * slope[half:, LANES:]).astype(jnp.bfloat16)


def grad_out(weight_t, packed, sources, blocks):
    cols, tokens = weight_t.shape[0], blocks[0].shape[0]
    vmem, whole = pl.BlockSpec(memory_space=pltpu.VMEM), pl.BlockSpec(memory_space=pl.ANY)
    return pl.pallas_call(
        grad_out_kernel,
        in_specs=[pl.BlockSpec(memory_space=pltpu.SMEM), vmem, vmem] + [whole] * len(blocks),
        out_specs=(vmem, vmem),
        out_shape=(
            jax.ShapeDtypeStruct((len(blocks), cols, tokens), jnp.bfloat16),
            jax.ShapeDtypeStruct((8, LANES), jnp.float32),
        ),
        scratch_shapes=[
            pltpu.VMEM((len(blocks), tokens, DW), jnp.bfloat16),
            pltpu.SemaphoreType.DMA((len(blocks),)),
        ],
        compiler_params=pltpu.CompilerParams(vmem_limit_bytes=VMEM),
        cost_estimate=HIDDEN,
    )(jnp.stack(sources), weight_t, packed, *blocks)


def add_products(totals_ref, width, grads, held, copies):
    tile, block = 256, 0
    terms = [grad_ref[i] for grad_ref in grads for i in range(grad_ref.shape[0])]
    for at in range(0, width, tile):
        part = slice(at, at + tile)
        total = jnp.zeros((totals_ref.shape[0], tile), jnp.float32)
        for i, term in enumerate(terms):
            if at == 0:
                copies[i].wait()
            total += jnp.dot(term, held[i, :, part], preferred_element_type=jnp.float32)
        totals_ref[:, part] = total


def early_kernel(groups, blocks, *refs):
    grads, blocks, (numer_ref, weight_ref, partner_ref) = refs[:groups], refs[groups : groups + blocks], refs[groups + blocks :][:3]
    out_ref, token_ref, weight_out_ref, held, sems = refs[-5:]
    copies = [pltpu.make_async_copy(block, held.at[i], sems.at[i]) for i, block in enumerate(blocks)]
    for copy in copies:
        copy.start()
    weight_out_ref[0] = 0.5 * (weight_ref[0] + partner_ref[0])
    token_ref[...] = jnp.zeros(token_ref.shape, token_ref.dtype)
    add_products(out_ref, out_ref.shape[1], grads, held, copies)
    out_ref[...] = numer_ref[...].astype(jnp.float32) - LEARN_RATE * (SCALE * out_ref[...])


def early_blocks(grads, blocks, numer_t, weight, partner_weight):
    vmem, smem = pl.BlockSpec(memory_space=pltpu.VMEM), pl.BlockSpec(memory_space=pltpu.SMEM)
    whole = pl.BlockSpec(memory_space=pl.ANY)
    return pl.pallas_call(
        partial(early_kernel, len(grads), len(blocks)),
        in_specs=[vmem] * len(grads) + [whole] * len(blocks) + [vmem, smem, smem],
        out_specs=(vmem, vmem, smem),
        out_shape=(
            jax.ShapeDtypeStruct(numer_t.shape, jnp.float32),
            jax.ShapeDtypeStruct((8, LANES), jnp.float32),
            jax.ShapeDtypeStruct((1,), jnp.float32),
        ),
        scratch_shapes=[
            pltpu.VMEM((len(blocks),) + blocks[0].shape, jnp.bfloat16),
            pltpu.SemaphoreType.DMA((len(blocks),)),
        ],
        compiler_params=pltpu.CompilerParams(vmem_limit_bytes=EARLY_VMEM),
        cost_estimate=HIDDEN,
    )(*grads, *blocks, numer_t, weight, partner_weight)


def late_kernel(groups, blocks, first, *refs):
    grads, blocks, early_ref = refs[:groups], refs[groups : groups + blocks], refs[groups + blocks]
    out_ref, held, early, total, sems = refs[-5:]
    width = out_ref.shape[1]
    columns = pl.ds(first, width)
    copies = [pltpu.make_async_copy(block.at[:, columns], held.at[i], sems.at[i]) for i, block in enumerate(blocks)]
    copies.append(pltpu.make_async_copy(early_ref.at[:, columns], early, sems.at[len(blocks)]))
    for copy in copies:
        copy.start()
    add_products(total, width, grads, held, copies)
    copies[-1].wait()
    out_ref[...] = (early[...] - LEARN_RATE * (SCALE * total[...])).astype(jnp.bfloat16)


def late_chunk(grads, blocks, early, first, width):
    cols = early.shape[0]
    tokens = blocks[0].shape[0]
    vmem, whole = pl.BlockSpec(memory_space=pltpu.VMEM), pl.BlockSpec(memory_space=pl.ANY)
    return pl.pallas_call(
        partial(late_kernel, len(grads), len(blocks), first),
        in_specs=[vmem] * len(grads) + [whole] * (len(blocks) + 1),
        out_specs=vmem,
        out_shape=jax.ShapeDtypeStruct((cols, width), jnp.bfloat16),
        scratch_shapes=[
            pltpu.VMEM((len(blocks), tokens, width), jnp.bfloat16),
            pltpu.VMEM((cols, width), jnp.float32),
            pltpu.VMEM((cols, width), jnp.float32),
            pltpu.SemaphoreType.DMA((len(blocks) + 1,)),
        ],
        compiler_params=pltpu.CompilerParams(vmem_limit_bytes=VMEM),
        cost_estimate=HIDDEN,
    )(*grads, *blocks, early)


def route(distance):
    devices = range(lax.axis_size("rep"))
    return [((i - distance) % len(devices), i) for i in devices]


def mix_with(hop_size, grads, blocks, early):
    pieces, first = [], 0
    for width in CHUNKS:
        local = late_chunk(grads, blocks, early, first, width)
        partner = lax.ppermute(local, "rep", route(hop_size))
        pieces.append((0.5 * local.astype(jnp.float32) + 0.5 * partner.astype(jnp.float32)).astype(jnp.bfloat16))
        first += width
    return jnp.concatenate(pieces, axis=1)


def weight_from(hop_size, weight):
    return lax.ppermute(weight, "rep", route(hop_size))


def per_hop(step_index, act, *operands):
    bit_count = lax.axis_size("rep").bit_length() - 1
    return lax.switch(step_index % bit_count, [partial(act, 2**bit) for bit in range(bit_count)], *operands)


def on_device(numerator, push_weight, norm_gain, activations, cotangent, step_index):
    count = lax.axis_size("fsdp")
    me = lax.axis_index("fsdp")
    core = me % 2
    ahead, back, far = ((me + step * (1 - 2 * core) + count) % count for step in (2, -2, 4))
    numer_t = numerator[0].T
    weight_t = (numer_t.astype(jnp.float32) / push_weight[0]).astype(jnp.bfloat16)
    own = norm(activations.reshape(-1, DW), norm_gain)
    first = to_chip(own, 1)
    third = to_chip(first, 1)
    packed = pack_cotangent(cotangent.reshape(-1, cotangent.shape[2]).T, count)
    partner_weight = per_hop(step_index, weight_from, scalar_after(push_weight, own))
    packed = copy_after(packed, own, partner_weight)
    packed = lax.all_to_all(packed, "fsdp", split_axis=0, concat_axis=0, tiled=True)
    second = to_chip(copy_after(own, packed), -1)
    blocks, grads = [], []
    for sources, block in (((me, me ^ 1), own), ((back, ahead ^ 1), first), ((far, far ^ 1), third)):
        pair = (block, to_core(block))
        blocks += pair
        grad, token = grad_out(weight_t, packed, sources, pair)
        grads.append(grad)
    early, token, new_weight = early_blocks(grads, blocks, numer_t, push_weight, partner_weight)
    second = once_there(second, token)
    blocks = [second, to_core(second)]
    grads = [grad_out(weight_t, packed, (s,), (b,))[0] for s, b in zip((ahead, back ^ 1), blocks)]
    mixed_t = per_hop(step_index, mix_with, grads, blocks, early)
    return mixed_t.T[None], new_weight


def solution(mesh):
    placed = (
        P("rep", None, "fsdp"),
        P("rep"),
        P(),
        P(None, ("rep", "fsdp"), None),
        P(None, ("rep", "fsdp"), None),
        P(),
    )
    return jax.shard_map(
        on_device,
        mesh=mesh,
        in_specs=placed,
        out_specs=(P("rep", None, "fsdp"), P("rep")),
        check_vma=False,
    )
```

```python
from functools import partial

import jax
import jax.numpy as jnp
from jax import lax
from jax.experimental import pallas as pl
from jax.experimental.pallas import tpu as pltpu
from jax.sharding import PartitionSpec as P

DW = 2560
LEARN_RATE = 1.5
EPSILON = 1e-05
SCALE = DW ** (-0.5)
LANES = 128
CHUNKS = (512, 768, 768, 512)
VMEM = 12 * 2**20
TILE = 256
HIDDEN = pl.CostEstimate(flops=1, bytes_accessed=1, transcendentals=0)


def pack_cotangent(cot_t, parts):
    cols, tokens = cot_t.shape
    cot_t = cot_t.reshape(parts, cols // parts, tokens)
    half = cols // parts // 2
    rest = cot_t[:, :, LANES:]
    gap = jnp.zeros((parts, half, LANES - 2 * (tokens - LANES)), cot_t.dtype)
    folded = jnp.concatenate([rest[:, :half], rest[:, half:], gap], axis=2)
    return jnp.concatenate([cot_t[:, :, :LANES], folded], axis=1)


def norm_kernel(tokens_ref, gain_ref, out_ref):
    wide = tokens_ref[...].astype(jnp.float32)
    mean_square = jnp.mean(wide * wide, axis=-1, keepdims=True)
    out_ref[...] = (wide * lax.rsqrt(mean_square + EPSILON) * gain_ref[...]).astype(jnp.bfloat16)


def norm(tokens, gain):
    return pl.pallas_call(
        norm_kernel,
        out_shape=jax.ShapeDtypeStruct(tokens.shape, jnp.bfloat16),
        compiler_params=pltpu.CompilerParams(vmem_limit_bytes=VMEM),
        cost_estimate=pl.CostEstimate(flops=8 * tokens.size, bytes_accessed=4 * tokens.size, transcendentals=0),
    )(tokens, gain[None])


def corner(array):
    return pl.BlockSpec((1,) * (array.ndim - 2) + (16, LANES), lambda i: (0,) * array.ndim)


def copy_kernel(array_ref, token_ref, out_ref):
    out_ref[...] = array_ref[...]


def copy_after(array, token):
    whole = pl.BlockSpec(array.shape, lambda i: (0,) * array.ndim)
    return pl.pallas_call(
        copy_kernel,
        grid=(1,),
        in_specs=[whole, corner(token)],
        out_specs=whole,
        out_shape=jax.ShapeDtypeStruct(array.shape, array.dtype),
        compiler_params=pltpu.CompilerParams(vmem_limit_bytes=VMEM),
        cost_estimate=HIDDEN,
    )(array, token)


def once_there(array, *tokens):
    whole = pl.BlockSpec(memory_space=pl.ANY)
    return pl.pallas_call(
        lambda *refs: None,
        in_specs=[whole] + [pl.BlockSpec(memory_space=pltpu.VMEM)] * len(tokens),
        out_specs=whole,
        out_shape=jax.ShapeDtypeStruct(array.shape, array.dtype),
        input_output_aliases={0: 0},
        compiler_params=pltpu.CompilerParams(vmem_limit_bytes=VMEM),
        cost_estimate=HIDDEN,
    )(array, *tokens)


def to_chip(values, step):
    count = lax.axis_size("fsdp")
    route = [(i, (i // 2 + (-step if i % 2 else step)) % (count // 2) * 2 + i % 2) for i in range(count)]
    return lax.ppermute(values, "fsdp", route)


def to_core(values):
    return lax.ppermute(values, "fsdp", [(i, i ^ 1) for i in range(lax.axis_size("fsdp"))])


def grad_out_kernel(ids_ref, weight_ref, cot_ref, *refs):
    blocks, out_ref = refs[:-1], refs[-1]
    _, cols, tokens = out_ref.shape
    half, rest = cols // 2, tokens - LANES
    for i, block in enumerate(blocks):
        pre_act = SCALE * lax.dot_general(
            weight_ref[...], block[...], (((1,), (1,)), ((), ())), preferred_element_type=jnp.float32
        )
        sig = jax.nn.sigmoid(pre_act)
        slope = sig * (1.0 + pre_act * (1.0 - sig))
        cot = cot_ref[ids_ref[i]]
        head = cot[:cols].astype(jnp.float32)
        tail = cot[cols:].astype(jnp.float32)
        out_ref[i, :, :LANES] = (head * slope[:, :LANES]).astype(jnp.bfloat16)
        out_ref[i, :half, LANES:] = (tail[:, :rest] * slope[:half, LANES:]).astype(jnp.bfloat16)
        out_ref[i, half:, LANES:] = (tail[:, rest : 2 * rest] * slope[half:, LANES:]).astype(jnp.bfloat16)


def grad_out(weight_t, packed, sources, blocks):
    cols, tokens = weight_t.shape[0], blocks[0].shape[0]
    vmem = pl.BlockSpec(memory_space=pltpu.VMEM)
    return pl.pallas_call(
        grad_out_kernel,
        in_specs=[pl.BlockSpec(memory_space=pltpu.SMEM)] + [vmem] * (2 + len(blocks)),
        out_specs=vmem,
        out_shape=jax.ShapeDtypeStruct((len(blocks), cols, tokens), jnp.bfloat16),
        compiler_params=pltpu.CompilerParams(vmem_limit_bytes=VMEM),
        cost_estimate=HIDDEN,
    )(jnp.stack(sources), weight_t, packed, *blocks)


def products(grads, blocks, columns):
    terms = [grad_ref[i] for grad_ref in grads for i in range(grad_ref.shape[0])]
    return sum(
        jnp.dot(term, block[:, columns], preferred_element_type=jnp.float32) for term, block in zip(terms, blocks)
    )


def early_kernel(groups, *refs):
    grads, blocks, (numer_ref, out_ref, token_ref) = refs[:groups], refs[groups:-3], refs[-3:]
    token_ref[...] = jnp.zeros(token_ref.shape, token_ref.dtype)
    for at in range(0, out_ref.shape[1], TILE):
        part = slice(at, at + TILE)
        update = LEARN_RATE * (SCALE * products(grads, blocks, part))
        out_ref[:, part] = numer_ref[:, part].astype(jnp.float32) - update


def early_blocks(grads, blocks, numer_t):
    vmem = pl.BlockSpec(memory_space=pltpu.VMEM)
    return pl.pallas_call(
        partial(early_kernel, len(grads)),
        in_specs=[vmem] * (len(grads) + len(blocks) + 1),
        out_specs=(vmem, vmem),
        out_shape=(
            jax.ShapeDtypeStruct(numer_t.shape, jnp.float32),
            jax.ShapeDtypeStruct((8, LANES), jnp.float32),
        ),
        compiler_params=pltpu.CompilerParams(vmem_limit_bytes=VMEM),
        cost_estimate=HIDDEN,
    )(*grads, *blocks, numer_t)


def late_kernel(groups, first, *refs):
    grads, blocks = refs[:groups], refs[groups:-4]
    early_ref, weight_ref, out_ref, weight_out_ref = refs[-4:]
    weight_out_ref[0] = weight_ref[0]
    for at in range(0, out_ref.shape[1], TILE):
        part = slice(first + at, first + at + TILE)
        update = LEARN_RATE * (SCALE * products(grads, blocks, part))
        out_ref[:, at : at + TILE] = (early_ref[:, part] - update).astype(jnp.bfloat16)


def late_chunk(grads, blocks, early, weight, first, width):
    vmem, smem = pl.BlockSpec(memory_space=pltpu.VMEM), pl.BlockSpec(memory_space=pltpu.SMEM)
    return pl.pallas_call(
        partial(late_kernel, len(grads), first),
        in_specs=[vmem] * (len(grads) + len(blocks) + 1) + [smem],
        out_specs=(vmem, smem),
        out_shape=(
            jax.ShapeDtypeStruct((early.shape[0], width), jnp.bfloat16),
            jax.ShapeDtypeStruct(weight.shape, weight.dtype),
        ),
        compiler_params=pltpu.CompilerParams(vmem_limit_bytes=VMEM),
        cost_estimate=HIDDEN,
    )(*grads, *blocks, early, weight)


def route(distance):
    devices = range(lax.axis_size("rep"))
    return [((i - distance) % len(devices), i) for i in devices]


def mix_with(hop_size, grads, blocks, early, weight):
    pieces, weights, first = [], [], 0
    for width in CHUNKS:
        local, handed_on = late_chunk(grads, blocks, early, weight, first, width)
        weights.append(handed_on)
        partner = lax.ppermute(local, "rep", route(hop_size))
        pieces.append((0.5 * local.astype(jnp.float32) + 0.5 * partner.astype(jnp.float32)).astype(jnp.bfloat16))
        first += width
    new_weight = 0.5 * (weight + lax.ppermute(weights[1], "rep", route(hop_size)))
    return jnp.concatenate(pieces, axis=1), new_weight


def per_hop(step_index, act, *operands):
    bit_count = lax.axis_size("rep").bit_length() - 1
    return lax.switch(step_index % bit_count, [partial(act, 2**bit) for bit in range(bit_count)], *operands)


def on_device(numerator, push_weight, norm_gain, activations, cotangent, step_index):
    count = lax.axis_size("fsdp")
    me = lax.axis_index("fsdp")
    core = me % 2
    ahead, back, far = ((me + step * (1 - 2 * core) + count) % count for step in (2, -2, 4))
    numer_t = numerator[0].T
    weight_t = (numer_t.astype(jnp.float32) / push_weight[0]).astype(jnp.bfloat16)
    own = norm(activations.reshape(-1, DW), norm_gain)
    first = to_chip(own, 1)
    third = to_chip(first, 1)
    packed = pack_cotangent(cotangent.reshape(-1, cotangent.shape[2]).T, count)
    packed = lax.all_to_all(packed, "fsdp", split_axis=0, concat_axis=0, tiled=True)
    second = to_chip(copy_after(own, packed), -1)
    blocks, grads = [], []
    for sources, block in (((me, me ^ 1), own), ((back, ahead ^ 1), first), ((ahead, back ^ 1), second)):
        pair = (block, to_core(block))
        blocks += pair
        grads.append(grad_out(weight_t, packed, sources, pair))
    early, token = early_blocks(grads, blocks, numer_t)
    third = once_there(third, token)
    blocks = [third, to_core(third)]
    grads = [grad_out(weight_t, packed, (s,), (b,)) for s, b in zip((far, far ^ 1), blocks)]
    mixed_t, new_weight = per_hop(step_index, mix_with, grads, blocks, early, push_weight)
    return mixed_t.T[None], new_weight


def solution(mesh):
    placed = (
        P("rep", None, "fsdp"),
        P("rep"),
        P(),
        P(None, ("rep", "fsdp"), None),
        P(None, ("rep", "fsdp"), None),
        P(),
    )
    return jax.shard_map(
        on_device,
        mesh=mesh,
        in_specs=placed,
        out_specs=(P("rep", None, "fsdp"), P("rep")),
        check_vma=False,
    )
```

```python
from functools import partial

import jax
import jax.numpy as jnp
from jax import lax
from jax.experimental import pallas as pl
from jax.experimental.pallas import tpu as pltpu
from jax.sharding import PartitionSpec as P

DW = 2560
LEARN_RATE = 1.5
EPSILON = 1e-05
SCALE = DW ** (-0.5)
LANES = 128
CHUNKS = (512, 768, 768, 512)
VMEM = 12 * 2**20
TILE = 256
COT_ROWS = 48
HIDDEN = pl.CostEstimate(flops=1, bytes_accessed=1, transcendentals=0)


def pack_cotangent(cot_t, parts):
    cols, tokens = cot_t.shape
    cot_t = cot_t.reshape(parts, cols // parts, tokens)
    half = cols // parts // 2
    rest = cot_t[:, :, LANES:]
    gap = jnp.zeros((parts, half, LANES - 2 * (tokens - LANES)), cot_t.dtype)
    folded = jnp.concatenate([rest[:, :half], rest[:, half:], gap], axis=2)
    return jnp.concatenate([cot_t[:, :, :LANES], folded], axis=1)


def prepare_kernel(ids_ref, tokens_ref, gain_ref, packed_ref, *out_refs):
    wide = tokens_ref[...].astype(jnp.float32)
    mean_square = jnp.mean(wide * wide, axis=-1, keepdims=True)
    normed = (wide * lax.rsqrt(mean_square + EPSILON) * gain_ref[...]).astype(jnp.bfloat16)
    place = 0
    for out_ref in out_refs:
        cots = out_ref.shape[0] // COT_ROWS - tokens_ref.shape[0] // COT_ROWS
        for slot in range(cots):
            chip = ids_ref[place]
            place += 1
            for part in range(packed_ref.shape[1] // COT_ROWS * 2):
                core, rows = divmod(part, packed_ref.shape[1] // COT_ROWS)
                out_ref[slot * COT_ROWS : (slot + 1) * COT_ROWS, part * LANES : (part + 1) * LANES] = packed_ref[
                    2 * chip + core, rows * COT_ROWS : (rows + 1) * COT_ROWS, :
                ]
        out_ref[cots * COT_ROWS :, :] = normed


def prepare(tokens, gain, packed, chips):
    vmem = pl.BlockSpec(memory_space=pltpu.VMEM)
    rows = [tokens.shape[0] + cots * COT_ROWS for cots in (2, 1, 1)]
    return pl.pallas_call(
        prepare_kernel,
        in_specs=[pl.BlockSpec(memory_space=pltpu.SMEM)] + [vmem] * 3,
        out_specs=[vmem] * 3,
        out_shape=[jax.ShapeDtypeStruct((r, DW), jnp.bfloat16) for r in rows],
        compiler_params=pltpu.CompilerParams(vmem_limit_bytes=VMEM),
        cost_estimate=HIDDEN,
    )(jnp.stack(chips), tokens, gain[None], packed)


def pass_on_kernel(message_ref, on_ref, kept_ref, sems):
    spare = on_ref.shape[0] - kept_ref.shape[0]
    tokens = message_ref.at[pl.ds(2 * COT_ROWS, message_ref.shape[0] - 2 * COT_ROWS)]
    moves = (
        (message_ref.at[pl.ds(0, COT_ROWS)], on_ref.at[pl.ds(spare, COT_ROWS)]),
        (tokens, on_ref.at[pl.ds(spare + COT_ROWS, tokens.shape[0])]),
        (message_ref.at[pl.ds(COT_ROWS, kept_ref.shape[0])], kept_ref),
    )
    copies = [pltpu.make_async_copy(*move, sems.at[i]) for i, move in enumerate(moves)]
    copies.append(pltpu.make_async_copy(message_ref.at[pl.ds(0, spare)], on_ref.at[pl.ds(0, spare)], sems.at[3]))
    for copy in copies:
        copy.start()
    for copy in copies:
        copy.wait()


def pass_on(message, spare=16):
    rows = message.shape[0] - COT_ROWS
    whole = pl.BlockSpec(memory_space=pl.ANY)
    return pl.pallas_call(
        pass_on_kernel,
        in_specs=[whole],
        out_specs=(whole, whole),
        out_shape=(
            jax.ShapeDtypeStruct((rows + spare, DW), message.dtype),
            jax.ShapeDtypeStruct((rows, DW), message.dtype),
        ),
        scratch_shapes=[pltpu.SemaphoreType.DMA((4,))],
        compiler_params=pltpu.CompilerParams(vmem_limit_bytes=VMEM),
        cost_estimate=HIDDEN,
    )(message)


def once_there(array, *tokens):
    whole = pl.BlockSpec(memory_space=pl.ANY)
    return pl.pallas_call(
        lambda *refs: None,
        in_specs=[whole] + [pl.BlockSpec(memory_space=pltpu.VMEM)] * len(tokens),
        out_specs=whole,
        out_shape=jax.ShapeDtypeStruct(array.shape, array.dtype),
        input_output_aliases={0: 0},
        compiler_params=pltpu.CompilerParams(vmem_limit_bytes=VMEM),
        cost_estimate=HIDDEN,
    )(array, *tokens)


def to_chip(values, step):
    count = lax.axis_size("fsdp")
    route = [(i, (i // 2 + (-step if i % 2 else step)) % (count // 2) * 2 + i % 2) for i in range(count)]
    return lax.ppermute(values, "fsdp", route)


def to_core(values):
    return lax.ppermute(values, "fsdp", [(i, i ^ 1) for i in range(lax.axis_size("fsdp"))])


def grad_out_kernel(core_ref, weight_ref, *refs):
    messages, (out_ref, token_ref) = refs[:-2], refs[-2:]
    _, cols, tokens = out_ref.shape
    half, rest = cols // 2, tokens - LANES
    token_ref[...] = jnp.zeros(token_ref.shape, token_ref.dtype)
    mine = pl.ds(pl.multiple_of(core_ref[0] * (DW // 2), LANES), DW // 2)
    for i, message in enumerate(messages):
        pre_act = SCALE * lax.dot_general(
            weight_ref[...], message[-tokens:, :], (((1,), (1,)), ((), ())), preferred_element_type=jnp.float32
        )
        sig = jax.nn.sigmoid(pre_act)
        slope = sig * (1.0 + pre_act * (1.0 - sig))
        at = message.shape[0] - tokens - COT_ROWS
        cot = message[at : at + COT_ROWS, mine]
        cot = jnp.concatenate([cot[:, at : at + LANES] for at in range(0, DW // 2, LANES)], axis=0)
        head = cot[:cols].astype(jnp.float32)
        tail = cot[cols:].astype(jnp.float32)
        out_ref[i, :, :LANES] = (head * slope[:, :LANES]).astype(jnp.bfloat16)
        out_ref[i, :half, LANES:] = (tail[:, :rest] * slope[:half, LANES:]).astype(jnp.bfloat16)
        out_ref[i, half:, LANES:] = (tail[:, rest : 2 * rest] * slope[half:, LANES:]).astype(jnp.bfloat16)


def grad_out(weight_t, core, tokens, messages):
    cols = weight_t.shape[0]
    vmem = pl.BlockSpec(memory_space=pltpu.VMEM)
    return pl.pallas_call(
        grad_out_kernel,
        in_specs=[pl.BlockSpec(memory_space=pltpu.SMEM)] + [vmem] * (1 + len(messages)),
        out_specs=(vmem, vmem),
        out_shape=(
            jax.ShapeDtypeStruct((len(messages), cols, tokens), jnp.bfloat16),
            jax.ShapeDtypeStruct((8, LANES), jnp.float32),
        ),
        compiler_params=pltpu.CompilerParams(vmem_limit_bytes=VMEM),
        cost_estimate=HIDDEN,
    )(core[None], weight_t, *messages)


def products(grads, blocks, columns):
    terms = [grad_ref[i] for grad_ref in grads for i in range(grad_ref.shape[0])]
    return sum(
        jnp.dot(term, block[-term.shape[1] :, columns], preferred_element_type=jnp.float32)
        for term, block in zip(terms, blocks)
    )


def early_kernel(groups, *refs):
    grads, blocks, (numer_ref, out_ref, token_ref) = refs[:groups], refs[groups:-3], refs[-3:]
    token_ref[...] = jnp.zeros(token_ref.shape, token_ref.dtype)
    for at in range(0, out_ref.shape[1], TILE):
        part = slice(at, at + TILE)
        update = LEARN_RATE * (SCALE * products(grads, blocks, part))
        out_ref[:, part] = numer_ref[:, part].astype(jnp.float32) - update


def early_blocks(grads, blocks, numer_t):
    vmem = pl.BlockSpec(memory_space=pltpu.VMEM)
    return pl.pallas_call(
        partial(early_kernel, len(grads)),
        in_specs=[vmem] * (len(grads) + len(blocks) + 1),
        out_specs=(vmem, vmem),
        out_shape=(
            jax.ShapeDtypeStruct(numer_t.shape, jnp.float32),
            jax.ShapeDtypeStruct((8, LANES), jnp.float32),
        ),
        compiler_params=pltpu.CompilerParams(vmem_limit_bytes=VMEM),
        cost_estimate=HIDDEN,
    )(*grads, *blocks, numer_t)


def late_kernel(groups, first, *refs):
    grads, blocks = refs[:groups], refs[groups:-7]
    early_ref, weight_ref, out_ref, weight_out_ref, held, early, sems = refs[-7:]
    tokens, width = held.shape[1:]
    columns = pl.ds(first, width)
    copies = [
        pltpu.make_async_copy(block.at[pl.ds(block.shape[0] - tokens, tokens), columns], held.at[i], sems.at[i])
        for i, block in enumerate(blocks)
    ]
    copies.append(pltpu.make_async_copy(early_ref.at[:, columns], early, sems.at[len(blocks)]))
    for copy in copies:
        copy.start()
    weight_out_ref[0] = weight_ref[0]
    for copy in copies:
        copy.wait()
    for at in range(0, width, TILE):
        part = slice(at, at + TILE)
        update = LEARN_RATE * (SCALE * products(grads, [held.at[i] for i in range(len(blocks))], part))
        out_ref[:, part] = (early[:, part] - update).astype(jnp.bfloat16)


def late_chunk(grads, blocks, early, weight, first, width):
    vmem, smem = pl.BlockSpec(memory_space=pltpu.VMEM), pl.BlockSpec(memory_space=pltpu.SMEM)
    whole = pl.BlockSpec(memory_space=pl.ANY)
    return pl.pallas_call(
        partial(late_kernel, len(grads), first),
        in_specs=[vmem] * len(grads) + [whole] * (len(blocks) + 1) + [smem],
        out_specs=(vmem, smem),
        out_shape=(
            jax.ShapeDtypeStruct((early.shape[0], width), jnp.bfloat16),
            jax.ShapeDtypeStruct(weight.shape, weight.dtype),
        ),
        scratch_shapes=[
            pltpu.VMEM((len(blocks), grads[0].shape[2], width), jnp.bfloat16),
            pltpu.VMEM((early.shape[0], width), jnp.float32),
            pltpu.SemaphoreType.DMA((len(blocks) + 1,)),
        ],
        compiler_params=pltpu.CompilerParams(vmem_limit_bytes=VMEM),
        cost_estimate=HIDDEN,
    )(*grads, *blocks, early, weight)


def route(distance):
    devices = range(lax.axis_size("rep"))
    return [((i - distance) % len(devices), i) for i in devices]


def mix_with(hop_size, grads, blocks, early, weight):
    pieces, weights, first = [], [], 0
    for width in CHUNKS:
        local, handed_on = late_chunk(grads, blocks, early, weight, first, width)
        weights.append(handed_on)
        partner = lax.ppermute(local, "rep", route(hop_size))
        pieces.append((0.5 * local.astype(jnp.float32) + 0.5 * partner.astype(jnp.float32)).astype(jnp.bfloat16))
        first += width
    new_weight = 0.5 * (weight + lax.ppermute(weights[1], "rep", route(hop_size)))
    return jnp.concatenate(pieces, axis=1), new_weight


def per_hop(step_index, act, *operands):
    bit_count = lax.axis_size("rep").bit_length() - 1
    return lax.switch(step_index % bit_count, [partial(act, 2**bit) for bit in range(bit_count)], *operands)


def on_device(numerator, push_weight, norm_gain, activations, cotangent, step_index):
    count = lax.axis_size("fsdp")
    me = lax.axis_index("fsdp")
    chip, core, chips = me // 2, me % 2, count // 2
    ahead, back, far = ((chip + step * (1 - 2 * core) + chips) % chips for step in (1, -1, 2))
    numer_t = numerator[0].T
    weight_t = (numer_t.astype(jnp.float32) / push_weight[0]).astype(jnp.bfloat16)
    packed = pack_cotangent(cotangent.reshape(-1, cotangent.shape[2]).T, count)
    tokens = activations.reshape(-1, DW)
    to_ahead, to_back, own = prepare(tokens, norm_gain, packed, (far, ahead, back, chip))
    grad_of = partial(grad_out, weight_t, core, tokens.shape[0])
    first = to_chip(to_ahead, 1)
    third, first = pass_on(first)
    third = to_chip(third, 1)
    blocks = [own, to_core(own)]
    grad_own, token = grad_of(blocks)
    second = to_chip(once_there(to_back, token), -1)
    grad_first, token = grad_of([first])
    first = once_there(first, token)
    received = [to_core(first), second, to_core(second)]
    grad_received, _ = grad_of(received)
    blocks += [first] + received
    early, token = early_blocks([grad_own, grad_first, grad_received], blocks, numer_t)
    third = once_there(third, token)
    blocks = [third, to_core(third)]
    grads = [grad_of([block])[0] for block in blocks]
    mixed_t, new_weight = per_hop(step_index, mix_with, grads, blocks, early, push_weight)
    return mixed_t.T[None], new_weight


def solution(mesh):
    placed = (
        P("rep", None, "fsdp"),
        P("rep"),
        P(),
        P(None, ("rep", "fsdp"), None),
        P(None, ("rep", "fsdp"), None),
        P(),
    )
    return jax.shard_map(
        on_device,
        mesh=mesh,
        in_specs=placed,
        out_specs=(P("rep", None, "fsdp"), P("rep")),
        check_vma=False,
    )
```

```python
from functools import partial

import jax
import jax.numpy as jnp
from jax import lax
from jax.experimental import pallas as pl
from jax.experimental.pallas import tpu as pltpu
from jax.sharding import PartitionSpec as P

DW = 2560
LEARN_RATE = 1.5
EPSILON = 1e-05
SCALE = DW ** (-0.5)
LANES = 128
CHUNKS = (512, 768, 768, 512)
VMEM = 12 * 2**20
TILE = 256
COT_ROWS = 48
HIDDEN = pl.CostEstimate(flops=1, bytes_accessed=1, transcendentals=0)


def pack_cotangent(cot_t, parts):
    cols, tokens = cot_t.shape
    cot_t = cot_t.reshape(parts, cols // parts, tokens)
    half = cols // parts // 2
    rest = cot_t[:, :, LANES:]
    gap = jnp.zeros((parts, half, LANES - 2 * (tokens - LANES)), cot_t.dtype)
    folded = jnp.concatenate([rest[:, :half], rest[:, half:], gap], axis=2)
    return jnp.concatenate([cot_t[:, :, :LANES], folded], axis=1)


def prepare_kernel(ids_ref, tokens_ref, gain_ref, packed_ref, *out_refs):
    wide = tokens_ref[...].astype(jnp.float32)
    mean_square = jnp.mean(wide * wide, axis=-1, keepdims=True)
    normed = (wide * lax.rsqrt(mean_square + EPSILON) * gain_ref[...]).astype(jnp.bfloat16)
    for place in range(ids_ref.shape[0]):
        out_ref, chip = out_refs[place], ids_ref[place]
        pieces = packed_ref.shape[1] // COT_ROWS
        for part in range(2 * pieces):
            core, rows = divmod(part, pieces)
            out_ref[:COT_ROWS, part * LANES : (part + 1) * LANES] = packed_ref[
                2 * chip + core, rows * COT_ROWS : (rows + 1) * COT_ROWS, :
            ]
    for out_ref in out_refs:
        if out_ref.shape[0] > COT_ROWS:
            out_ref[-normed.shape[0] :, :] = normed


def prepare(tokens, gain, packed, chips):
    vmem = pl.BlockSpec(memory_space=pltpu.VMEM)
    count = tokens.shape[0]
    rows = (COT_ROWS + count, COT_ROWS + count, COT_ROWS, COT_ROWS, count)
    return pl.pallas_call(
        prepare_kernel,
        in_specs=[pl.BlockSpec(memory_space=pltpu.SMEM)] + [vmem] * 3,
        out_specs=[vmem] * len(rows),
        out_shape=[jax.ShapeDtypeStruct((r, DW), jnp.bfloat16) for r in rows],
        compiler_params=pltpu.CompilerParams(vmem_limit_bytes=VMEM),
        cost_estimate=HIDDEN,
    )(jnp.stack(chips), tokens, gain[None], packed)


def once_there(array, token):
    whole = pl.BlockSpec(memory_space=pl.ANY)
    corner = (1,) * (token.ndim - 2) + (min(16, token.shape[-2]), LANES)
    return pl.pallas_call(
        lambda *refs: None,
        grid=(1,),
        in_specs=[whole, pl.BlockSpec(corner, lambda i: (0,) * token.ndim)],
        out_specs=whole,
        out_shape=jax.ShapeDtypeStruct(array.shape, array.dtype),
        input_output_aliases={0: 0},
        compiler_params=pltpu.CompilerParams(vmem_limit_bytes=VMEM),
        cost_estimate=HIDDEN,
    )(array, token)


def tail_kernel(array_ref, token_ref, out_ref, sem):
    rows = out_ref.shape[0]
    copy = pltpu.make_async_copy(array_ref.at[pl.ds(array_ref.shape[0] - rows, rows)], out_ref, sem)
    copy.start()
    copy.wait()


def tail_after(array, rows, token):
    whole = pl.BlockSpec(memory_space=pl.ANY)
    return pl.pallas_call(
        tail_kernel,
        in_specs=[whole, pl.BlockSpec(memory_space=pltpu.VMEM)],
        out_specs=whole,
        out_shape=jax.ShapeDtypeStruct((rows, array.shape[1]), array.dtype),
        scratch_shapes=[pltpu.SemaphoreType.DMA],
        compiler_params=pltpu.CompilerParams(vmem_limit_bytes=VMEM),
        cost_estimate=HIDDEN,
    )(array, token)


def to_chip(values, step):
    count = lax.axis_size("fsdp")
    route = [(i, (i // 2 + (-step if i % 2 else step)) % (count // 2) * 2 + i % 2) for i in range(count)]
    return lax.ppermute(values, "fsdp", route)


def to_core(values):
    return lax.ppermute(values, "fsdp", [(i, i ^ 1) for i in range(lax.axis_size("fsdp"))])


def grad_out_kernel(plan, core_ref, weight_ref, *refs):
    arrays, (out_ref, token_ref) = refs[:-2], refs[-2:]
    _, cols, tokens = out_ref.shape
    half, rest = cols // 2, tokens - LANES
    token_ref[...] = jnp.zeros(token_ref.shape, token_ref.dtype)
    mine = pl.ds(pl.multiple_of(core_ref[0] * (DW // 2), LANES), DW // 2)
    for i, (message, columns, at) in enumerate(plan):
        pre_act = SCALE * lax.dot_general(
            weight_ref[...], arrays[message][-tokens:, :], (((1,), (1,)), ((), ())), preferred_element_type=jnp.float32
        )
        sig = jax.nn.sigmoid(pre_act)
        slope = sig * (1.0 + pre_act * (1.0 - sig))
        cot = arrays[columns][at : at + COT_ROWS, mine]
        cot = jnp.concatenate([cot[:, lane : lane + LANES] for lane in range(0, DW // 2, LANES)], axis=0)
        head = cot[:cols].astype(jnp.float32)
        tail = cot[cols:].astype(jnp.float32)
        out_ref[i, :, :LANES] = (head * slope[:, :LANES]).astype(jnp.bfloat16)
        out_ref[i, :half, LANES:] = (tail[:, :rest] * slope[:half, LANES:]).astype(jnp.bfloat16)
        out_ref[i, half:, LANES:] = (tail[:, rest : 2 * rest] * slope[half:, LANES:]).astype(jnp.bfloat16)


def grad_out(weight_t, core, tokens, pairs):
    cols = weight_t.shape[0]
    arrays, plan = [], []
    for message, columns, at in pairs:
        for array in (message, columns):
            if not any(array is other for other in arrays):
                arrays.append(array)
        place = [next(i for i, other in enumerate(arrays) if other is array) for array in (message, columns)]
        plan.append((*place, at))
    vmem = pl.BlockSpec(memory_space=pltpu.VMEM)
    return pl.pallas_call(
        partial(grad_out_kernel, plan),
        in_specs=[pl.BlockSpec(memory_space=pltpu.SMEM)] + [vmem] * (1 + len(arrays)),
        out_specs=(vmem, vmem),
        out_shape=(
            jax.ShapeDtypeStruct((len(pairs), cols, tokens), jnp.bfloat16),
            jax.ShapeDtypeStruct((8, LANES), jnp.float32),
        ),
        compiler_params=pltpu.CompilerParams(vmem_limit_bytes=VMEM),
        cost_estimate=HIDDEN,
    )(core[None], weight_t, *arrays)


def products(grads, blocks, columns):
    terms = [grad_ref[i] for grad_ref in grads for i in range(grad_ref.shape[0])]
    return sum(
        jnp.dot(term, block[-term.shape[1] :, columns], preferred_element_type=jnp.float32)
        for term, block in zip(terms, blocks)
    )


def early_kernel(groups, *refs):
    grads, blocks, (numer_ref, out_ref, token_ref) = refs[:groups], refs[groups:-3], refs[-3:]
    token_ref[...] = jnp.zeros(token_ref.shape, token_ref.dtype)
    for at in range(0, out_ref.shape[1], TILE):
        part = slice(at, at + TILE)
        update = LEARN_RATE * (SCALE * products(grads, blocks, part))
        out_ref[:, part] = numer_ref[:, part].astype(jnp.float32) - update


def early_blocks(grads, blocks, numer_t):
    vmem = pl.BlockSpec(memory_space=pltpu.VMEM)
    return pl.pallas_call(
        partial(early_kernel, len(grads)),
        in_specs=[vmem] * (len(grads) + len(blocks) + 1),
        out_specs=(vmem, vmem),
        out_shape=(
            jax.ShapeDtypeStruct(numer_t.shape, jnp.float32),
            jax.ShapeDtypeStruct((8, LANES), jnp.float32),
        ),
        compiler_params=pltpu.CompilerParams(vmem_limit_bytes=VMEM),
        cost_estimate=HIDDEN,
    )(*grads, *blocks, numer_t)


def late_kernel(groups, first, *refs):
    grads, blocks = refs[:groups], refs[groups:-7]
    early_ref, weight_ref, out_ref, weight_out_ref, held, early, sems = refs[-7:]
    tokens, width = held.shape[1:]
    columns = pl.ds(first, width)
    copies = [
        pltpu.make_async_copy(block.at[pl.ds(block.shape[0] - tokens, tokens), columns], held.at[i], sems.at[i])
        for i, block in enumerate(blocks)
    ]
    copies.append(pltpu.make_async_copy(early_ref.at[:, columns], early, sems.at[len(blocks)]))
    for copy in copies:
        copy.start()
    weight_out_ref[0] = weight_ref[0]
    for copy in copies:
        copy.wait()
    for at in range(0, width, TILE):
        part = slice(at, at + TILE)
        update = LEARN_RATE * (SCALE * products(grads, [held.at[i] for i in range(len(blocks))], part))
        out_ref[:, part] = (early[:, part] - update).astype(jnp.bfloat16)


def late_chunk(grads, blocks, early, weight, first, width):
    vmem, smem = pl.BlockSpec(memory_space=pltpu.VMEM), pl.BlockSpec(memory_space=pltpu.SMEM)
    whole = pl.BlockSpec(memory_space=pl.ANY)
    return pl.pallas_call(
        partial(late_kernel, len(grads), first),
        in_specs=[vmem] * len(grads) + [whole] * (len(blocks) + 1) + [smem],
        out_specs=(vmem, smem),
        out_shape=(
            jax.ShapeDtypeStruct((early.shape[0], width), jnp.bfloat16),
            jax.ShapeDtypeStruct(weight.shape, weight.dtype),
        ),
        scratch_shapes=[
            pltpu.VMEM((len(blocks), grads[0].shape[2], width), jnp.bfloat16),
            pltpu.VMEM((early.shape[0], width), jnp.float32),
            pltpu.SemaphoreType.DMA((len(blocks) + 1,)),
        ],
        compiler_params=pltpu.CompilerParams(vmem_limit_bytes=VMEM),
        cost_estimate=HIDDEN,
    )(*grads, *blocks, early, weight)


def route(distance):
    devices = range(lax.axis_size("rep"))
    return [((i - distance) % len(devices), i) for i in devices]


def mix_with(hop_size, grads, blocks, early, weight):
    pieces, weights, first = [], [], 0
    for width in CHUNKS:
        local, handed_on = late_chunk(grads, blocks, early, weight, first, width)
        weights.append(handed_on)
        partner = lax.ppermute(local, "rep", route(hop_size))
        pieces.append((0.5 * local.astype(jnp.float32) + 0.5 * partner.astype(jnp.float32)).astype(jnp.bfloat16))
        first += width
    new_weight = 0.5 * (weight + lax.ppermute(weights[1], "rep", route(hop_size)))
    return jnp.concatenate(pieces, axis=1), new_weight


def per_hop(step_index, act, *operands):
    bit_count = lax.axis_size("rep").bit_length() - 1
    return lax.switch(step_index % bit_count, [partial(act, 2**bit) for bit in range(bit_count)], *operands)


def on_device(numerator, push_weight, norm_gain, activations, cotangent, step_index):
    count = lax.axis_size("fsdp")
    me = lax.axis_index("fsdp")
    chip, core, chips = me // 2, me % 2, count // 2
    ahead, back, far = ((chip + step * (1 - 2 * core) + chips) % chips for step in (1, -1, 2))
    numer_t = numerator[0].T
    weight_t = (numer_t.astype(jnp.float32) / push_weight[0]).astype(jnp.bfloat16)
    packed = pack_cotangent(cotangent.reshape(-1, cotangent.shape[2]).T, count)
    tokens = activations.reshape(-1, DW)
    own, to_far, cot_ahead, cot_back, plain = prepare(tokens, norm_gain, packed, (chip, far, ahead, back))
    grad_of = partial(grad_out, weight_t, core, tokens.shape[0])
    first = to_chip(to_far, 1)
    third = to_chip(first, 1)
    cot_ahead = to_chip(cot_ahead, 1)
    cot_back = to_chip(cot_back, -1)
    cots = jnp.concatenate([cot_ahead, cot_back])
    twin_cots = to_core(cots)
    twin = to_core(own)
    grad_own, _ = grad_of([(own, own, 0), (twin, twin, 0)])
    second = to_chip(once_there(plain, twin_cots), -1)
    grad_first, token = grad_of([(first, cot_ahead, 0)])
    first = tail_after(first, tokens.shape[0], token)
    twin_first, twin_second = to_core(first), to_core(second)
    grad_received, _ = grad_of([(twin_first, twin_cots, 0), (second, cots, COT_ROWS), (twin_second, twin_cots, COT_ROWS)])
    blocks = [own, twin, first, twin_first, second, twin_second]
    early, token = early_blocks([grad_own, grad_first, grad_received], blocks, numer_t)
    third = once_there(third, token)
    blocks = [third, to_core(third)]
    grads = [grad_of([(block, block, 0)])[0] for block in blocks]
    mixed_t, new_weight = per_hop(step_index, mix_with, grads, blocks, early, push_weight)
    return mixed_t.T[None], new_weight


def solution(mesh):
    placed = (
        P("rep", None, "fsdp"),
        P("rep"),
        P(),
        P(None, ("rep", "fsdp"), None),
        P(None, ("rep", "fsdp"), None),
        P(),
    )
    return jax.shard_map(
        on_device,
        mesh=mesh,
        in_specs=placed,
        out_specs=(P("rep", None, "fsdp"), P("rep")),
        check_vma=False,
    )
```

```python
from functools import partial

import jax
import jax.numpy as jnp
from jax import lax
from jax.experimental import pallas as pl
from jax.experimental.pallas import tpu as pltpu
from jax.sharding import PartitionSpec as P

DW = 2560
LEARN_RATE = 1.5
EPSILON = 1e-05
SCALE = DW ** (-0.5)
LANES = 128
CHUNKS = (512, 768, 768, 512)
VMEM = 12 * 2**20
TILE = 256
HIDDEN = pl.CostEstimate(flops=1, bytes_accessed=1, transcendentals=0)


def pack_cotangent(cot_t, parts):
    cols, tokens = cot_t.shape
    cot_t = cot_t.reshape(parts, cols // parts, tokens)
    half = cols // parts // 2
    rest = cot_t[:, :, LANES:]
    gap = jnp.zeros((parts, half, LANES - 2 * (tokens - LANES)), cot_t.dtype)
    folded = jnp.concatenate([rest[:, :half], rest[:, half:], gap], axis=2)
    return jnp.concatenate([cot_t[:, :, :LANES], folded], axis=1)


def norm_kernel(tokens_ref, gain_ref, *out_refs):
    wide = tokens_ref[...].astype(jnp.float32)
    mean_square = jnp.mean(wide * wide, axis=-1, keepdims=True)
    normed = (wide * lax.rsqrt(mean_square + EPSILON) * gain_ref[...]).astype(jnp.bfloat16)
    for out_ref in out_refs:
        out_ref[...] = normed


def norm(tokens, gain):
    vmem = pl.BlockSpec(memory_space=pltpu.VMEM)
    return pl.pallas_call(
        norm_kernel,
        in_specs=[vmem, vmem],
        out_specs=(vmem, vmem),
        out_shape=(jax.ShapeDtypeStruct(tokens.shape, jnp.bfloat16),) * 2,
        compiler_params=pltpu.CompilerParams(vmem_limit_bytes=VMEM),
        cost_estimate=pl.CostEstimate(flops=8 * tokens.size, bytes_accessed=4 * tokens.size, transcendentals=0),
    )(tokens, gain[None])


def corner(array):
    return pl.BlockSpec(
        (1,) * (array.ndim - 2) + (min(16, array.shape[-2]), LANES), lambda i: (0,) * array.ndim
    )


def once_there(array, *tokens):
    whole = pl.BlockSpec(memory_space=pl.ANY)
    return pl.pallas_call(
        lambda *refs: None,
        grid=(1,),
        in_specs=[whole] + [corner(token) for token in tokens],
        out_specs=whole,
        out_shape=jax.ShapeDtypeStruct(array.shape, array.dtype),
        input_output_aliases={0: 0},
        compiler_params=pltpu.CompilerParams(vmem_limit_bytes=VMEM),
        cost_estimate=HIDDEN,
    )(array, *tokens)


def to_chip(values, step):
    count = lax.axis_size("fsdp")
    route = [(i, (i // 2 + (-step if i % 2 else step)) % (count // 2) * 2 + i % 2) for i in range(count)]
    return lax.ppermute(values, "fsdp", route)


def to_core(values):
    return lax.ppermute(values, "fsdp", [(i, i ^ 1) for i in range(lax.axis_size("fsdp"))])


def grad_out_kernel(ids_ref, weight_ref, cot_ref, *refs):
    blocks, out_ref = refs[:-1], refs[-1]
    _, cols, tokens = out_ref.shape
    half, rest = cols // 2, tokens - LANES
    for i, block in enumerate(blocks):
        pre_act = SCALE * lax.dot_general(
            weight_ref[...], block[...], (((1,), (1,)), ((), ())), preferred_element_type=jnp.float32
        )
        sig = jax.nn.sigmoid(pre_act)
        slope = sig * (1.0 + pre_act * (1.0 - sig))
        cot = cot_ref[ids_ref[i]]
        head = cot[:cols].astype(jnp.float32)
        tail = cot[cols:].astype(jnp.float32)
        out_ref[i, :, :LANES] = (head * slope[:, :LANES]).astype(jnp.bfloat16)
        out_ref[i, :half, LANES:] = (tail[:, :rest] * slope[:half, LANES:]).astype(jnp.bfloat16)
        out_ref[i, half:, LANES:] = (tail[:, rest : 2 * rest] * slope[half:, LANES:]).astype(jnp.bfloat16)


def grad_out(weight_t, packed, sources, blocks):
    cols, tokens = weight_t.shape[0], blocks[0].shape[0]
    vmem = pl.BlockSpec(memory_space=pltpu.VMEM)
    return pl.pallas_call(
        grad_out_kernel,
        in_specs=[pl.BlockSpec(memory_space=pltpu.SMEM)] + [vmem] * (2 + len(blocks)),
        out_specs=vmem,
        out_shape=jax.ShapeDtypeStruct((len(blocks), cols, tokens), jnp.bfloat16),
        compiler_params=pltpu.CompilerParams(vmem_limit_bytes=VMEM),
        cost_estimate=HIDDEN,
    )(jnp.stack(sources), weight_t, packed, *blocks)


def products(grads, blocks, columns):
    terms = [grad_ref[i] for grad_ref in grads for i in range(grad_ref.shape[0])]
    return sum(
        jnp.dot(term, block[-term.shape[1] :, columns], preferred_element_type=jnp.float32)
        for term, block in zip(terms, blocks)
    )


def early_kernel(groups, *refs):
    grads, blocks, (numer_ref, out_ref, token_ref) = refs[:groups], refs[groups:-3], refs[-3:]
    token_ref[...] = jnp.zeros(token_ref.shape, token_ref.dtype)
    for at in range(0, out_ref.shape[1], TILE):
        part = slice(at, at + TILE)
        update = LEARN_RATE * (SCALE * products(grads, blocks, part))
        out_ref[:, part] = numer_ref[:, part].astype(jnp.float32) - update


def early_blocks(grads, blocks, numer_t):
    vmem = pl.BlockSpec(memory_space=pltpu.VMEM)
    return pl.pallas_call(
        partial(early_kernel, len(grads)),
        in_specs=[vmem] * (len(grads) + len(blocks) + 1),
        out_specs=(vmem, vmem),
        out_shape=(
            jax.ShapeDtypeStruct(numer_t.shape, jnp.float32),
            jax.ShapeDtypeStruct((8, LANES), jnp.float32),
        ),
        compiler_params=pltpu.CompilerParams(vmem_limit_bytes=VMEM),
        cost_estimate=HIDDEN,
    )(*grads, *blocks, numer_t)


def late_kernel(groups, first, *refs):
    grads, blocks = refs[:groups], refs[groups:-7]
    early_ref, weight_ref, out_ref, weight_out_ref, held, early, sems = refs[-7:]
    tokens, width = held.shape[1:]
    columns = pl.ds(first, width)
    copies = [
        pltpu.make_async_copy(block.at[pl.ds(block.shape[0] - tokens, tokens), columns], held.at[i], sems.at[i])
        for i, block in enumerate(blocks)
    ]
    copies.append(pltpu.make_async_copy(early_ref.at[:, columns], early, sems.at[len(blocks)]))
    for copy in copies:
        copy.start()
    weight_out_ref[0] = weight_ref[0]
    for copy in copies:
        copy.wait()
    for at in range(0, width, TILE):
        part = slice(at, at + TILE)
        update = LEARN_RATE * (SCALE * products(grads, [held.at[i] for i in range(len(blocks))], part))
        out_ref[:, part] = (early[:, part] - update).astype(jnp.bfloat16)


def late_chunk(grads, blocks, early, weight, first, width):
    vmem, smem = pl.BlockSpec(memory_space=pltpu.VMEM), pl.BlockSpec(memory_space=pltpu.SMEM)
    whole = pl.BlockSpec(memory_space=pl.ANY)
    return pl.pallas_call(
        partial(late_kernel, len(grads), first),
        in_specs=[vmem] * len(grads) + [whole] * (len(blocks) + 1) + [smem],
        out_specs=(vmem, smem),
        out_shape=(
            jax.ShapeDtypeStruct((early.shape[0], width), jnp.bfloat16),
            jax.ShapeDtypeStruct(weight.shape, weight.dtype),
        ),
        scratch_shapes=[
            pltpu.VMEM((len(blocks), grads[0].shape[2], width), jnp.bfloat16),
            pltpu.VMEM((early.shape[0], width), jnp.float32),
            pltpu.SemaphoreType.DMA((len(blocks) + 1,)),
        ],
        compiler_params=pltpu.CompilerParams(vmem_limit_bytes=VMEM),
        cost_estimate=HIDDEN,
    )(*grads, *blocks, early, weight)


def route(distance):
    devices = range(lax.axis_size("rep"))
    return [((i - distance) % len(devices), i) for i in devices]


def mix_with(hop_size, grads, blocks, early, weight):
    pieces, weights, first = [], [], 0
    for width in CHUNKS:
        local, handed_on = late_chunk(grads, blocks, early, weight, first, width)
        weights.append(handed_on)
        partner = lax.ppermute(local, "rep", route(hop_size))
        pieces.append((0.5 * local.astype(jnp.float32) + 0.5 * partner.astype(jnp.float32)).astype(jnp.bfloat16))
        first += width
    new_weight = 0.5 * (weight + lax.ppermute(weights[1], "rep", route(hop_size)))
    return jnp.concatenate(pieces, axis=1), new_weight


def per_hop(step_index, act, *operands):
    bit_count = lax.axis_size("rep").bit_length() - 1
    return lax.switch(step_index % bit_count, [partial(act, 2**bit) for bit in range(bit_count)], *operands)


def on_device(numerator, push_weight, norm_gain, activations, cotangent, step_index):
    count = lax.axis_size("fsdp")
    me = lax.axis_index("fsdp")
    core = me % 2
    ahead, back, far = ((me + step * (1 - 2 * core) + count) % count for step in (2, -2, 4))
    numer_t = numerator[0].T
    weight_t = (numer_t.astype(jnp.float32) / push_weight[0]).astype(jnp.bfloat16)
    own, plain = norm(activations.reshape(-1, DW), norm_gain)
    first = to_chip(own, 1)
    third = to_chip(first, 1)
    packed = pack_cotangent(cotangent.reshape(-1, cotangent.shape[2]).T, count)
    packed = lax.all_to_all(packed, "fsdp", split_axis=0, concat_axis=0, tiled=True)
    second = to_chip(once_there(plain, packed), -1)
    blocks, grads = [], []
    for sources, block in (((me, me ^ 1), own), ((back, ahead ^ 1), first), ((ahead, back ^ 1), second)):
        pair = (block, to_core(block))
        blocks += pair
        grads.append(grad_out(weight_t, packed, sources, pair))
    early, token = early_blocks(grads, blocks, numer_t)
    third = once_there(third, token)
    blocks = [third, to_core(third)]
    grads = [grad_out(weight_t, packed, (s,), (b,)) for s, b in zip((far, far ^ 1), blocks)]
    mixed_t, new_weight = per_hop(step_index, mix_with, grads, blocks, early, push_weight)
    return mixed_t.T[None], new_weight


def solution(mesh):
    placed = (
        P("rep", None, "fsdp"),
        P("rep"),
        P(),
        P(None, ("rep", "fsdp"), None),
        P(None, ("rep", "fsdp"), None),
        P(),
    )
    return jax.shard_map(
        on_device,
        mesh=mesh,
        in_specs=placed,
        out_specs=(P("rep", None, "fsdp"), P("rep")),
        check_vma=False,
    )
```

```python
from functools import partial

import jax
import jax.numpy as jnp
from jax import lax
from jax.experimental import pallas as pl
from jax.experimental.pallas import tpu as pltpu
from jax.sharding import PartitionSpec as P

DW = 2560
LEARN_RATE = 1.5
EPSILON = 1e-05
SCALE = DW ** (-0.5)
LANES = 128
CHUNKS = (512, 768, 768, 512)
VMEM = 12 * 2**20
TILE = 256
X_SIZE, Y_SIZE = 4, 8
HIDDEN = pl.CostEstimate(flops=1, bytes_accessed=1, transcendentals=0)


def pack_cotangent(cot_t, parts):
    cols, tokens = cot_t.shape
    cot_t = cot_t.reshape(parts, cols // parts, tokens)
    half = cols // parts // 2
    rest = cot_t[:, :, LANES:]
    gap = jnp.zeros((parts, half, LANES - 2 * (tokens - LANES)), cot_t.dtype)
    folded = jnp.concatenate([rest[:, :half], rest[:, half:], gap], axis=2)
    return jnp.concatenate([cot_t[:, :, :LANES], folded], axis=1)


def norm_kernel(tokens_ref, gain_ref, *out_refs):
    wide = tokens_ref[...].astype(jnp.float32)
    mean_square = jnp.mean(wide * wide, axis=-1, keepdims=True)
    normed = (wide * lax.rsqrt(mean_square + EPSILON) * gain_ref[...]).astype(jnp.bfloat16)
    for out_ref in out_refs:
        out_ref[...] = normed


def norm(tokens, gain):
    vmem = pl.BlockSpec(memory_space=pltpu.VMEM)
    return pl.pallas_call(
        norm_kernel,
        in_specs=[vmem, vmem],
        out_specs=(vmem, vmem),
        out_shape=(jax.ShapeDtypeStruct(tokens.shape, jnp.bfloat16),) * 2,
        compiler_params=pltpu.CompilerParams(vmem_limit_bytes=VMEM),
        cost_estimate=pl.CostEstimate(flops=8 * tokens.size, bytes_accessed=4 * tokens.size, transcendentals=0),
    )(tokens, gain[None])


def corner(array):
    return pl.BlockSpec(
        (1,) * (array.ndim - 2) + (min(16, array.shape[-2]), LANES), lambda i: (0,) * array.ndim
    )


def once_there(array, *tokens):
    whole = pl.BlockSpec(memory_space=pl.ANY)
    return pl.pallas_call(
        lambda *refs: None,
        grid=(1,),
        in_specs=[whole] + [corner(token) for token in tokens],
        out_specs=whole,
        out_shape=jax.ShapeDtypeStruct(array.shape, array.dtype),
        input_output_aliases={0: 0},
        compiler_params=pltpu.CompilerParams(vmem_limit_bytes=VMEM),
        cost_estimate=HIDDEN,
    )(array, *tokens)


def to_chip(values, step):
    count = lax.axis_size("fsdp")
    route = [(i, (i // 2 + (-step if i % 2 else step)) % (count // 2) * 2 + i % 2) for i in range(count)]
    return lax.ppermute(values, "fsdp", route)


def to_core(values):
    return lax.ppermute(values, "fsdp", [(i, i ^ 1) for i in range(lax.axis_size("fsdp"))])


def grad_out_kernel(ids_ref, weight_ref, cot_ref, *refs):
    blocks, out_ref = refs[:-1], refs[-1]
    _, cols, tokens = out_ref.shape
    half, rest = cols // 2, tokens - LANES
    for i, block in enumerate(blocks):
        pre_act = SCALE * lax.dot_general(
            weight_ref[...], block[...], (((1,), (1,)), ((), ())), preferred_element_type=jnp.float32
        )
        sig = jax.nn.sigmoid(pre_act)
        slope = sig * (1.0 + pre_act * (1.0 - sig))
        cot = cot_ref[ids_ref[i]]
        head = cot[:cols].astype(jnp.float32)
        tail = cot[cols:].astype(jnp.float32)
        out_ref[i, :, :LANES] = (head * slope[:, :LANES]).astype(jnp.bfloat16)
        out_ref[i, :half, LANES:] = (tail[:, :rest] * slope[:half, LANES:]).astype(jnp.bfloat16)
        out_ref[i, half:, LANES:] = (tail[:, rest : 2 * rest] * slope[half:, LANES:]).astype(jnp.bfloat16)


def grad_out(weight_t, packed, sources, blocks):
    cols, tokens = weight_t.shape[0], blocks[0].shape[0]
    vmem = pl.BlockSpec(memory_space=pltpu.VMEM)
    return pl.pallas_call(
        grad_out_kernel,
        in_specs=[pl.BlockSpec(memory_space=pltpu.SMEM)] + [vmem] * (2 + len(blocks)),
        out_specs=vmem,
        out_shape=jax.ShapeDtypeStruct((len(blocks), cols, tokens), jnp.bfloat16),
        compiler_params=pltpu.CompilerParams(vmem_limit_bytes=VMEM),
        cost_estimate=HIDDEN,
    )(jnp.stack(sources), weight_t, packed, *blocks)


def products(grads, blocks, columns):
    terms = [grad_ref[i] for grad_ref in grads for i in range(grad_ref.shape[0])]
    return sum(
        jnp.dot(term, block[-term.shape[1] :, columns], preferred_element_type=jnp.float32)
        for term, block in zip(terms, blocks)
    )


def early_kernel(groups, *refs):
    grads, blocks, (numer_ref, out_ref, token_ref) = refs[:groups], refs[groups:-3], refs[-3:]
    token_ref[...] = jnp.zeros(token_ref.shape, token_ref.dtype)
    for at in range(0, out_ref.shape[1], TILE):
        part = slice(at, at + TILE)
        update = LEARN_RATE * (SCALE * products(grads, blocks, part))
        out_ref[:, part] = (numer_ref[:, part].astype(jnp.float32) - update).astype(jnp.bfloat16)


def early_blocks(grads, blocks, numer_t):
    vmem = pl.BlockSpec(memory_space=pltpu.VMEM)
    return pl.pallas_call(
        partial(early_kernel, len(grads)),
        in_specs=[vmem] * (len(grads) + len(blocks) + 1),
        out_specs=(vmem, vmem),
        out_shape=(
            jax.ShapeDtypeStruct(numer_t.shape, jnp.bfloat16),
            jax.ShapeDtypeStruct((8, LANES), jnp.float32),
        ),
        compiler_params=pltpu.CompilerParams(vmem_limit_bytes=VMEM),
        cost_estimate=HIDDEN,
    )(*grads, *blocks, numer_t)


def late_kernel(groups, first, *refs):
    grads, blocks = refs[:groups], refs[groups:-7]
    early_ref, weight_ref, out_ref, weight_out_ref, held, early, sems = refs[-7:]
    tokens, width = held.shape[1:]
    columns = pl.ds(first, width)
    copies = [
        pltpu.make_async_copy(block.at[pl.ds(block.shape[0] - tokens, tokens), columns], held.at[i], sems.at[i])
        for i, block in enumerate(blocks)
    ]
    copies.append(pltpu.make_async_copy(early_ref.at[:, columns], early, sems.at[len(blocks)]))
    for copy in copies:
        copy.start()
    weight_out_ref[0] = weight_ref[0]
    for copy in copies:
        copy.wait()
    for at in range(0, width, TILE):
        part = slice(at, at + TILE)
        update = LEARN_RATE * (SCALE * products(grads, [held.at[i] for i in range(len(blocks))], part))
        out_ref[:, part] = (early[:, part].astype(jnp.float32) - update).astype(jnp.bfloat16)


def late_chunk(grads, blocks, early, weight, first, width):
    vmem, smem = pl.BlockSpec(memory_space=pltpu.VMEM), pl.BlockSpec(memory_space=pltpu.SMEM)
    whole = pl.BlockSpec(memory_space=pl.ANY)
    return pl.pallas_call(
        partial(late_kernel, len(grads), first),
        in_specs=[vmem] * len(grads) + [whole] * (len(blocks) + 1) + [smem],
        out_specs=(vmem, smem),
        out_shape=(
            jax.ShapeDtypeStruct((early.shape[0], width), jnp.bfloat16),
            jax.ShapeDtypeStruct(weight.shape, weight.dtype),
        ),
        scratch_shapes=[
            pltpu.VMEM((len(blocks), grads[0].shape[2], width), jnp.bfloat16),
            pltpu.VMEM((early.shape[0], width), early.dtype),
            pltpu.SemaphoreType.DMA((len(blocks) + 1,)),
        ],
        compiler_params=pltpu.CompilerParams(vmem_limit_bytes=VMEM),
        cost_estimate=HIDDEN,
    )(*grads, *blocks, early, weight)


def route(distance):
    devices = range(lax.axis_size("rep"))
    return [((i - distance) % len(devices), i) for i in devices]


def from_partner(values, hop_size, backwards):
    if not backwards:
        return lax.ppermute(values, "rep", route(hop_size))
    count = lax.axis_size("rep")
    column, layer = X_SIZE, X_SIZE * Y_SIZE
    midway = [i // layer * layer + (i - 3 * column) % layer for i in range(count)]
    values = lax.ppermute(values, "rep", list(enumerate(midway)))
    return lax.ppermute(values, "rep", [(midway[i], (i + hop_size) % count) for i in range(count)])


def mix_with(hop_size, grads, blocks, early, weight):
    pieces, weights, first = [], [], 0
    for width in CHUNKS:
        local, handed_on = late_chunk(grads, blocks, early, weight, first, width)
        weights.append(handed_on)
        partner = from_partner(local, hop_size, hop_size == 2 * X_SIZE and first == 0)
        pieces.append((0.5 * local.astype(jnp.float32) + 0.5 * partner.astype(jnp.float32)).astype(jnp.bfloat16))
        first += width
    new_weight = 0.5 * (weight + lax.ppermute(weights[1], "rep", route(hop_size)))
    return jnp.concatenate(pieces, axis=1), new_weight


def per_hop(step_index, act, *operands):
    bit_count = lax.axis_size("rep").bit_length() - 1
    return lax.switch(step_index % bit_count, [partial(act, 2**bit) for bit in range(bit_count)], *operands)


def on_device(numerator, push_weight, norm_gain, activations, cotangent, step_index):
    count = lax.axis_size("fsdp")
    me = lax.axis_index("fsdp")
    core = me % 2
    ahead, back, far = ((me + step * (1 - 2 * core) + count) % count for step in (2, -2, 4))
    numer_t = numerator[0].T
    weight_t = (numer_t.astype(jnp.float32) / push_weight[0]).astype(jnp.bfloat16)
    own, plain = norm(activations.reshape(-1, DW), norm_gain)
    first = to_chip(own, 1)
    third = to_chip(first, 1)
    packed = pack_cotangent(cotangent.reshape(-1, cotangent.shape[2]).T, count)
    packed = lax.all_to_all(packed, "fsdp", split_axis=0, concat_axis=0, tiled=True)
    second = to_chip(once_there(plain, packed), -1)
    blocks, grads = [], []
    for sources, block in (((me, me ^ 1), own), ((back, ahead ^ 1), first), ((ahead, back ^ 1), second)):
        pair = (block, to_core(block))
        blocks += pair
        grads.append(grad_out(weight_t, packed, sources, pair))
    early, token = early_blocks(grads, blocks, numer_t)
    third = once_there(third, token)
    blocks = [third, to_core(third)]
    grads = [grad_out(weight_t, packed, (s,), (b,)) for s, b in zip((far, far ^ 1), blocks)]
    mixed_t, new_weight = per_hop(step_index, mix_with, grads, blocks, early, push_weight)
    return mixed_t.T[None], new_weight


def solution(mesh):
    placed = (
        P("rep", None, "fsdp"),
        P("rep"),
        P(),
        P(None, ("rep", "fsdp"), None),
        P(None, ("rep", "fsdp"), None),
        P(),
    )
    return jax.shard_map(
        on_device,
        mesh=mesh,
        in_specs=placed,
        out_specs=(P("rep", None, "fsdp"), P("rep")),
        check_vma=False,
    )
```

```python
from functools import partial

import jax
import jax.numpy as jnp
from jax import lax
from jax.experimental import pallas as pl
from jax.experimental.pallas import tpu as pltpu
from jax.sharding import PartitionSpec as P

DW = 2560
LEARN_RATE = 1.5
EPSILON = 1e-05
SCALE = DW ** (-0.5)
LANES = 128
CHUNKS = (512, 768, 768, 512)
VMEM = 12 * 2**20
TILE = 256
X_SIZE, Y_SIZE = 4, 8
HIDDEN = pl.CostEstimate(flops=1, bytes_accessed=1, transcendentals=0)


def pack_cotangent(cot_t, parts):
    cols, tokens = cot_t.shape
    cot_t = cot_t.reshape(parts, cols // parts, tokens)
    half = cols // parts // 2
    rest = cot_t[:, :, LANES:]
    gap = jnp.zeros((parts, half, LANES - 2 * (tokens - LANES)), cot_t.dtype)
    folded = jnp.concatenate([rest[:, :half], rest[:, half:], gap], axis=2)
    return jnp.concatenate([cot_t[:, :, :LANES], folded], axis=1)


def norm_kernel(tokens_ref, gain_ref, *out_refs):
    wide = tokens_ref[...].astype(jnp.float32)
    mean_square = jnp.mean(wide * wide, axis=-1, keepdims=True)
    normed = (wide * lax.rsqrt(mean_square + EPSILON) * gain_ref[...]).astype(jnp.bfloat16)
    for out_ref in out_refs:
        out_ref[...] = normed


def norm(tokens, gain):
    vmem = pl.BlockSpec(memory_space=pltpu.VMEM)
    return pl.pallas_call(
        norm_kernel,
        in_specs=[vmem, vmem],
        out_specs=(vmem, vmem),
        out_shape=(jax.ShapeDtypeStruct(tokens.shape, jnp.bfloat16),) * 2,
        compiler_params=pltpu.CompilerParams(vmem_limit_bytes=VMEM),
        cost_estimate=pl.CostEstimate(flops=8 * tokens.size, bytes_accessed=4 * tokens.size, transcendentals=0),
    )(tokens, gain[None])


def corner(array):
    return pl.BlockSpec(
        (1,) * (array.ndim - 2) + (min(16, array.shape[-2]), LANES), lambda i: (0,) * array.ndim
    )


def once_there(array, *tokens):
    whole = pl.BlockSpec(memory_space=pl.ANY)
    return pl.pallas_call(
        lambda *refs: None,
        grid=(1,),
        in_specs=[whole] + [corner(token) for token in tokens],
        out_specs=whole,
        out_shape=jax.ShapeDtypeStruct(array.shape, array.dtype),
        input_output_aliases={0: 0},
        compiler_params=pltpu.CompilerParams(vmem_limit_bytes=VMEM),
        cost_estimate=HIDDEN,
    )(array, *tokens)


def to_chip(values, step):
    count = lax.axis_size("fsdp")
    route = [(i, (i // 2 + (-step if i % 2 else step)) % (count // 2) * 2 + i % 2) for i in range(count)]
    return lax.ppermute(values, "fsdp", route)


def to_core(values):
    return lax.ppermute(values, "fsdp", [(i, i ^ 1) for i in range(lax.axis_size("fsdp"))])


def grad_out_kernel(ids_ref, weight_ref, cot_ref, *refs):
    blocks, out_ref = refs[:-1], refs[-1]
    _, cols, tokens = out_ref.shape
    half, rest = cols // 2, tokens - LANES
    for i, block in enumerate(blocks):
        pre_act = SCALE * lax.dot_general(
            weight_ref[...], block[...], (((1,), (1,)), ((), ())), preferred_element_type=jnp.float32
        )
        sig = jax.nn.sigmoid(pre_act)
        slope = sig * (1.0 + pre_act * (1.0 - sig))
        cot = cot_ref[ids_ref[i]]
        head = cot[:cols].astype(jnp.float32)
        tail = cot[cols:].astype(jnp.float32)
        out_ref[i, :, :LANES] = (head * slope[:, :LANES]).astype(jnp.bfloat16)
        out_ref[i, :half, LANES:] = (tail[:, :rest] * slope[:half, LANES:]).astype(jnp.bfloat16)
        out_ref[i, half:, LANES:] = (tail[:, rest : 2 * rest] * slope[half:, LANES:]).astype(jnp.bfloat16)


def grad_out(weight_t, packed, sources, blocks):
    cols, tokens = weight_t.shape[0], blocks[0].shape[0]
    vmem = pl.BlockSpec(memory_space=pltpu.VMEM)
    return pl.pallas_call(
        grad_out_kernel,
        in_specs=[pl.BlockSpec(memory_space=pltpu.SMEM)] + [vmem] * (2 + len(blocks)),
        out_specs=vmem,
        out_shape=jax.ShapeDtypeStruct((len(blocks), cols, tokens), jnp.bfloat16),
        compiler_params=pltpu.CompilerParams(vmem_limit_bytes=VMEM),
        cost_estimate=HIDDEN,
    )(jnp.stack(sources), weight_t, packed, *blocks)


def products(grads, blocks, columns):
    terms = [grad_ref[i] for grad_ref in grads for i in range(grad_ref.shape[0])]
    return sum(
        jnp.dot(term, block[-term.shape[1] :, columns], preferred_element_type=jnp.float32)
        for term, block in zip(terms, blocks)
    )


def early_kernel(groups, *refs):
    grads, blocks, (numer_ref, out_ref, token_ref) = refs[:groups], refs[groups:-3], refs[-3:]
    token_ref[...] = jnp.zeros(token_ref.shape, token_ref.dtype)
    for at in range(0, out_ref.shape[1], TILE):
        part = slice(at, at + TILE)
        update = LEARN_RATE * (SCALE * products(grads, blocks, part))
        out_ref[:, part] = (numer_ref[:, part].astype(jnp.float32) - update).astype(jnp.bfloat16)


def early_blocks(grads, blocks, numer_t):
    vmem = pl.BlockSpec(memory_space=pltpu.VMEM)
    return pl.pallas_call(
        partial(early_kernel, len(grads)),
        in_specs=[vmem] * (len(grads) + len(blocks) + 1),
        out_specs=(vmem, vmem),
        out_shape=(
            jax.ShapeDtypeStruct(numer_t.shape, jnp.bfloat16),
            jax.ShapeDtypeStruct((8, LANES), jnp.float32),
        ),
        compiler_params=pltpu.CompilerParams(vmem_limit_bytes=VMEM),
        cost_estimate=HIDDEN,
    )(*grads, *blocks, numer_t)


def late_kernel(groups, first, *refs):
    grads, blocks = refs[:groups], refs[groups:-7]
    early_ref, weight_ref, out_ref, weight_out_ref, held, early, sems = refs[-7:]
    tokens, width = held.shape[1:]
    columns = pl.ds(first, width)
    copies = [
        pltpu.make_async_copy(block.at[pl.ds(block.shape[0] - tokens, tokens), columns], held.at[i], sems.at[i])
        for i, block in enumerate(blocks)
    ]
    copies.append(pltpu.make_async_copy(early_ref.at[:, columns], early, sems.at[len(blocks)]))
    for copy in copies:
        copy.start()
    weight_out_ref[0] = weight_ref[0]
    for copy in copies:
        copy.wait()
    for at in range(0, width, TILE):
        part = slice(at, at + TILE)
        update = LEARN_RATE * (SCALE * products(grads, [held.at[i] for i in range(len(blocks))], part))
        out_ref[:, part] = (early[:, part].astype(jnp.float32) - update).astype(jnp.bfloat16)


def late_chunk(grads, blocks, early, weight, first, width):
    vmem, smem = pl.BlockSpec(memory_space=pltpu.VMEM), pl.BlockSpec(memory_space=pltpu.SMEM)
    whole = pl.BlockSpec(memory_space=pl.ANY)
    return pl.pallas_call(
        partial(late_kernel, len(grads), first),
        in_specs=[vmem] * len(grads) + [whole] * (len(blocks) + 1) + [smem],
        out_specs=(vmem, smem),
        out_shape=(
            jax.ShapeDtypeStruct((early.shape[0], width), jnp.bfloat16),
            jax.ShapeDtypeStruct(weight.shape, weight.dtype),
        ),
        scratch_shapes=[
            pltpu.VMEM((len(blocks), grads[0].shape[2], width), jnp.bfloat16),
            pltpu.VMEM((early.shape[0], width), early.dtype),
            pltpu.SemaphoreType.DMA((len(blocks) + 1,)),
        ],
        compiler_params=pltpu.CompilerParams(vmem_limit_bytes=VMEM),
        cost_estimate=HIDDEN,
    )(*grads, *blocks, early, weight)


def route(distance):
    devices = range(lax.axis_size("rep"))
    return [((i - distance) % len(devices), i) for i in devices]


def from_partner(values, hop_size, backwards):
    if not backwards:
        return lax.ppermute(values, "rep", route(hop_size))
    count = lax.axis_size("rep")
    column, layer = X_SIZE, X_SIZE * Y_SIZE
    midway = [i // layer * layer + (i - 3 * column) % layer for i in range(count)]
    values = lax.ppermute(values, "rep", list(enumerate(midway)))
    return lax.ppermute(values, "rep", [(midway[i], (i + hop_size) % count) for i in range(count)])


def mix_with(hop_size, grads, blocks, early, weight):
    pieces, weights, first = [], [], 0
    for width in CHUNKS:
        local, handed_on = late_chunk(grads, blocks, early, weight, first, width)
        weights.append(handed_on)
        partner = from_partner(local, hop_size, hop_size == 2 * X_SIZE and first == 0)
        pieces.append((0.5 * local.astype(jnp.float32) + 0.5 * partner.astype(jnp.float32)).astype(jnp.bfloat16))
        first += width
    new_weight = 0.5 * (weight + lax.ppermute(weights[1], "rep", route(hop_size)))
    return jnp.concatenate(pieces, axis=1), new_weight


def per_hop(step_index, act, *operands):
    bit_count = lax.axis_size("rep").bit_length() - 1
    return lax.switch(step_index % bit_count, [partial(act, 2**bit) for bit in range(bit_count)], *operands)


def on_device(numerator, push_weight, norm_gain, activations, cotangent, step_index):
    count = lax.axis_size("fsdp")
    me = lax.axis_index("fsdp")
    core = me % 2
    ahead, back, far = ((me + step * (1 - 2 * core) + count) % count for step in (2, -2, 4))
    numer_t = numerator[0].T
    weight_t = (numer_t.astype(jnp.float32) / push_weight[0]).astype(jnp.bfloat16)
    own, plain = norm(activations.reshape(-1, DW), norm_gain)
    first = to_chip(own, 1)
    third = to_chip(first, 1)
    packed = pack_cotangent(cotangent.reshape(-1, cotangent.shape[2]).T, count)
    packed = lax.all_to_all(packed, "fsdp", split_axis=0, concat_axis=0, tiled=True)
    second = to_chip(plain, -1)
    blocks, grads = [], []
    for sources, block in (((me, me ^ 1), own), ((back, ahead ^ 1), first), ((ahead, back ^ 1), second)):
        pair = (block, to_core(block))
        blocks += pair
        grads.append(grad_out(weight_t, packed, sources, pair))
    early, token = early_blocks(grads, blocks, numer_t)
    third = once_there(third, token)
    blocks = [third, to_core(third)]
    grads = [grad_out(weight_t, packed, (s,), (b,)) for s, b in zip((far, far ^ 1), blocks)]
    mixed_t, new_weight = per_hop(step_index, mix_with, grads, blocks, early, push_weight)
    return mixed_t.T[None], new_weight


def solution(mesh):
    placed = (
        P("rep", None, "fsdp"),
        P("rep"),
        P(),
        P(None, ("rep", "fsdp"), None),
        P(None, ("rep", "fsdp"), None),
        P(),
    )
    return jax.shard_map(
        on_device,
        mesh=mesh,
        in_specs=placed,
        out_specs=(P("rep", None, "fsdp"), P("rep")),
        check_vma=False,
    )
```
